512 devices in a mesh: rep: 8 (over x, z_hi), ty: 8 (over z_lo), tx: 8 (over y, core).
Axes of the slice: x: 4, y: 4, z: 16 (z_hi: 2, z_lo: 8; z = z_hi * 8 + z_lo), core: 2. Of those that a mesh axis runs over, the one named last changes fastest.
Arguments:
- features: bfloat16 [8, 128, 1536, 128], P('rep', 'ty', 'tx'), may hold values from -6 to 6
- fine_grad: bfloat16 [8, 128, 1536, 128], P('rep', 'ty', 'tx'), may hold values from -6 to 6
- conv_weight: bfloat16 [3, 3, 128, 128], replicated, may hold values from -0.1875 to 0.1875
- bottom: bfloat16 [8, 256, 512], P('rep', ('ty', 'tx')), may hold values from -12 to 12
- bottom_grad: bfloat16 [8, 256, 512], P('rep', ('ty', 'tx')), may hold values from -6 to 6
- query_weight: bfloat16 [512, 512], replicated, may hold values from -0.25 to 0.25
- key_weight: bfloat16 [512, 512], replicated, may hold values from -0.25 to 0.25
- value_weight: bfloat16 [512, 512], replicated, may hold values from -0.25 to 0.25
Outputs:
- feature_grad: bfloat16 [8, 128, 1536, 128], P('rep', 'ty', 'tx')
- conv_weight_grad: float32 [3, 3, 128, 128], replicated
- bottom_input_grad: bfloat16 [8, 256, 512], P('rep', ('ty', 'tx'))
- projection_grad: float32 [512, 1536], P(('ty', 'tx'))
The draws below stay inside these ranges and needn't reach their ends.
All inputs are finite; a program needn't handle non-finite values.
Results may differ from the reference program's by a relative error of at most 0.015.
The reference program's roundings to bfloat16 on the way (of `activation`, `probs_low`, `dscores_low` and `proj_grads`) count: a program that leaves them out, or rounds other values in their place, can miss the bound.
Values may be sent and summed in bfloat16 or wider, within the bound.
A program may use at most 64 MiB of HBM per device.

```python
import math
import jax
import jax.numpy as jnp
from jax import lax

C = 128
D_ATT = 512
HEAD_DIM = 64
BOTTOM = 256
IMAGES = 8
H = 128
W = 1536


def draw_bottom(key, part):
    key = jax.random.fold_in(key, 11)
    key_base = jax.random.fold_in(key, 0)
    shape = (IMAGES, BOTTOM, D_ATT)
    drawn = jax.random.normal(key_base, shape, jnp.float32)
    return jnp.clip(drawn, -12.0, 12.0).astype(jnp.bfloat16)


def level_of(own_key, dims, cuts, smallest, top_value):
    def one(dim, shards_of):
        draws = jax.random.uniform(jax.random.fold_in(jax.random.fold_in(own_key, 6), dim), (shards_of,), jnp.float32, smallest / len(cuts), top_value / len(cuts))
        return jnp.repeat(jnp.exp(draws), dims[dim] // shards_of).reshape((-1,) + (1,) * (len(dims) - dim - 1))

    loudness = one(*cuts[0])
    for cut in cuts[1:]:
        loudness = loudness * one(*cut)
    return loudness


def gaussian(key, shape, deviation, reach, cuts=(), held_as=jnp.bfloat16):
    array = deviation * jax.random.normal(key, shape, jnp.float32)
    if cuts:
        array = array * level_of(key, shape, cuts, -0.22, 0.18)
    return jnp.clip(array, -reach, reach).astype(held_as)


def setup_inputs(seed: int = 0) -> dict:
    key_list = jax.random.split(jax.random.key(seed), 9)
    features = gaussian(key_list[0], (IMAGES, H, W, C), 1.0, 6.0, ((0, 8), (1, 8), (2, 8)))
    fine_grad = gaussian(key_list[1], (IMAGES, H, W, C), 1.0, 6.0, ((0, 8), (1, 8), (2, 8)))
    conv_weight = gaussian(key_list[2], (3, 3, C, C), (9 * C) ** -0.5, 0.1875)
    bottom = draw_bottom(jax.random.fold_in(key_list[8], 71), 0)
    bottom_grad = gaussian(key_list[4], (IMAGES, BOTTOM, D_ATT), 1.0, 6.0, ((0, 8), (1, 64)))
    query_weight = gaussian(key_list[5], (D_ATT, D_ATT), D_ATT ** -0.5, 0.25)
    key_weight = gaussian(key_list[6], (D_ATT, D_ATT), D_ATT ** -0.5, 0.25)
    value_weight = gaussian(key_list[7], (D_ATT, D_ATT), D_ATT ** -0.5, 0.25)
    return dict(features=features, fine_grad=fine_grad, conv_weight=conv_weight, bottom=bottom, bottom_grad=bottom_grad, query_weight=query_weight, key_weight=key_weight, value_weight=value_weight)


def attention_back(query, key_rows, value_rows, upstream, head_size):
    rows = query.shape[0]
    count = key_rows.shape[0]
    width = query.shape[1]
    head_count = width // head_size
    query_heads = query.reshape(rows, head_count, head_size).astype(jnp.float32)
    key_heads = key_rows.reshape(count, head_count, head_size).astype(jnp.float32)
    value_heads = value_rows.reshape(count, head_count, head_size).astype(jnp.float32)
    upstream_heads = upstream.reshape(rows, head_count, head_size).astype(jnp.float32)
    score_scale = 1.0 / math.sqrt(head_size)
    scores = jnp.einsum('rhe,she->hrs', query_heads, key_heads) * score_scale
    highest = lax.optimization_barrier(jnp.max(scores, axis=-1, keepdims=True))
    expos = jnp.exp(scores - highest)
    probs = expos / lax.optimization_barrier(jnp.sum(expos, axis=-1, keepdims=True))
    probs_low = lax.optimization_barrier(probs.astype(jnp.bfloat16)).astype(jnp.float32)
    dprobs = jnp.einsum('rhe,she->hrs', upstream_heads, value_heads)
    value_grad = jnp.einsum('hrs,rhe->she', probs_low, upstream_heads)
    dscores = probs * (dprobs - lax.optimization_barrier(jnp.sum(dprobs * probs, axis=-1, keepdims=True)))
    dscores_low = lax.optimization_barrier((dscores * score_scale).astype(jnp.bfloat16)).astype(jnp.float32)
    query_grad = jnp.einsum('hrs,she->rhe', dscores_low, key_heads)
    key_grad = jnp.einsum('hrs,rhe->she', dscores_low, query_heads)
    return (query_grad.reshape(rows, width), key_grad.reshape(count, width), value_grad.reshape(count, width))

def fine_image(pair, conv_weight):
    image, upstream = pair
    rows, cols, chans = image.shape
    image_f = image.astype(jnp.float32)
    gate_value = jax.nn.sigmoid(image_f)
    activation = (image_f * gate_value).astype(jnp.bfloat16)
    act_slope = gate_value * (1.0 + image_f * (1.0 - gate_value))
    act_pad = jnp.pad(activation, ((1, 1), (1, 1), (0, 0)))
    grad_pad = jnp.pad(upstream, ((1, 1), (1, 1), (0, 0)))
    act_cat = jnp.concatenate([act_pad[row_off:row_off + rows, col_off:col_off + cols] for row_off in range(3) for col_off in range(3)], axis=-1).reshape(rows * cols, 9 * chans)
    grad_cat = jnp.concatenate([grad_pad[2 - row_off:2 - row_off + rows, 2 - col_off:2 - col_off + cols] for row_off in range(3) for col_off in range(3)], axis=-1).reshape(rows * cols, 9 * chans)
    weight_part = lax.dot_general(act_cat, upstream.reshape(rows * cols, chans), (((0,), (0,)), ((), ())), preferred_element_type=jnp.float32)
    flipped = conv_weight.transpose(0, 1, 3, 2).reshape(9 * chans, chans)
    act_grad = jnp.dot(grad_cat, flipped, preferred_element_type=jnp.float32).reshape(rows, cols, chans)
    feature_grad = (upstream.astype(jnp.float32) + act_slope * act_grad).astype(jnp.bfloat16)
    return (feature_grad, weight_part)

def bottom_image(pair, query_weight, key_weight, value_weight):
    tokens, token_grad = pair
    query = jnp.dot(tokens, query_weight, preferred_element_type=jnp.float32).astype(jnp.bfloat16)
    key_rows = jnp.dot(tokens, key_weight, preferred_element_type=jnp.float32).astype(jnp.bfloat16)
    value_rows = jnp.dot(tokens, value_weight, preferred_element_type=jnp.float32).astype(jnp.bfloat16)
    query_grad, key_grad, value_grad = attention_back(query, key_rows, value_rows, token_grad, HEAD_DIM)
    proj_grads = jnp.concatenate((query_grad, key_grad, value_grad), axis=1).astype(jnp.bfloat16)
    joined = jnp.concatenate((query_weight, key_weight, value_weight), axis=1)
    back = lax.dot_general(proj_grads, joined, (((1,), (1,)), ((), ())), preferred_element_type=jnp.float32)
    token_out = (token_grad.astype(jnp.float32) + back).astype(jnp.bfloat16)
    weight_part = lax.dot_general(tokens, proj_grads, (((0,), (0,)), ((), ())), preferred_element_type=jnp.float32)
    return (token_out, weight_part)

def reference(features, fine_grad, conv_weight, bottom, bottom_grad, query_weight, key_weight, value_weight):
    feature_grad, conv_parts = lax.map(lambda pair: fine_image(pair, conv_weight), (features, fine_grad))
    conv_weight_grad = lax.optimization_barrier(jnp.sum(conv_parts, axis=0)).reshape(3, 3, conv_weight.shape[2], conv_weight.shape[3])
    bottom_input_grad, proj_parts = lax.map(lambda pair: bottom_image(pair, query_weight, key_weight, value_weight), (bottom, bottom_grad))
    projection_grad = lax.optimization_barrier(jnp.sum(proj_parts, axis=0))
    return (feature_grad, conv_weight_grad, bottom_input_grad, projection_grad)
```

```python
import dataclasses
import functools

import jax
import jax.numpy as jnp
from jax import lax
from jax.experimental import pallas as pl
from jax.experimental.pallas import tpu as pltpu
from jax.sharding import PartitionSpec as P

HEAD_DIM = 64
LANES = 128
TILE = 16
MESH = pl.DeviceIdType.MESH
BF16 = jnp.bfloat16
F32 = jnp.float32

NN = (((1,), (0,)), ((), ()))
NT = (((1,), (1,)), ((), ()))
TN = (((0,), (0,)), ((), ()))


def dot(a, b, dims):
    return lax.dot_general(a, b, dims, preferred_element_type=F32)


@dataclasses.dataclass(frozen=True)
class Dims:
    x: int
    zh: int
    ty: int
    tx: int
    rows: int
    cols: int
    tok: int
    width: int

    @property
    def z(self):
        return self.zh * self.ty

    @property
    def part(self):
        return 9 * LANES // self.tx

    @property
    def owners(self):
        return 9 if self.z >= 9 else 3

    @property
    def piece(self):
        return self.part // self.owners

    @property
    def tokens(self):
        return self.ty * self.tx * self.tok

    def owner(self, j):
        return j * self.z // self.owners


def message_slots(d):
    slots = {}
    count = 0
    for name, n in (
        ("row", 2),
        ("col", 6),
        ("tok_z", d.ty),
        ("tok_t", d.tx),
        ("scatter", d.tx),
        ("sum_x", d.x),
        ("own", max(d.owners, d.z)),
        ("cast", max(d.owners, d.z)),
        ("gather", d.tx),
        ("proj_z", d.zh),
        ("proj_x", d.x),
    ):
        slots[name] = count
        count += n
    return slots, count


def kernel(
    d,
    features,
    fine_grad,
    conv_weight,
    bottom,
    bottom_grad,
    query_weight,
    key_weight,
    value_weight,
    feature_out,
    weight_out,
    token_out,
    proj_out,
    feat_v,
    grad_v,
    shifted,
    taps,
    proj_w,
    out_v,
    acc,
    part_v,
    scatter_v,
    sum_v,
    total_v,
    own_v,
    fin,
    col_send,
    col_recv,
    col_halo,
    tok_v,
    pack_v,
    gath,
    wide,
    tok_all,
    qkv,
    pgrad,
    pz_v,
    px_v,
    local_sem,
    send_sem,
    recv_sem,
):
    slots, _ = message_slots(d)
    rows, cols = d.rows, d.cols
    rep, ty, tx = (lax.axis_index(a) for a in ("rep", "ty", "tx"))
    x, zh = rep // d.zh, rep % d.zh
    z = zh * d.ty + ty

    def at_x(i):
        return (lax.rem(x + i, d.x) * d.zh + zh, ty, tx)

    def at_z(k):
        return (x * d.zh + k // d.ty, lax.rem(k, d.ty), tx)

    def at_tx(t):
        return (rep, ty, t)

    def at_ty(t):
        return (rep, t, tx)

    def send(src, dst, name, out_index, in_index, device):
        return pltpu.make_async_remote_copy(
            src_ref=src,
            dst_ref=dst,
            send_sem=send_sem.at[slots[name] + out_index],
            recv_sem=recv_sem.at[slots[name] + in_index],
            device_id=device,
            device_id_type=MESH,
        )

    sent = []

    def start(copy, when=None):
        sent.append((when, copy))
        if when is None:
            copy.start()
        else:
            pl.when(when)(copy.start)

    def local(src, dst, i):
        copy = pltpu.make_async_copy(src, dst, local_sem.at[i])
        copy.start()
        return copy

    in_tok = [local(bottom.at[0], tok_v.at[0], 0), local(bottom_grad.at[0], tok_v.at[1], 1)]
    in_grad = local(fine_grad.at[0], grad_v.at[pl.ds(1, rows)], 2)
    in_feat = local(features.at[0], feat_v, 3)
    in_proj = [
        local(w, proj_w.at[i], 4 + i) for i, w in enumerate((query_weight, key_weight, value_weight))
    ]
    in_taps = [
        local(conv_weight.at[k // 3, k % 3], taps.at[:, pl.ds(k * LANES, LANES)], 7 + k)
        for k in range(9)
    ]

    barrier = pltpu.get_barrier_semaphore()
    peers = [at_tx(lax.rem(tx + i, d.tx)) for i in range(1, d.tx)]
    peers += [at_x(i) for i in range(1, d.x)]
    peers += [at_z(lax.rem(z + i, d.z)) for i in range(1, d.z)]
    for dy in (1, d.ty - 1):
        for dx in (1, d.tx - 1):
            peers.append((rep, lax.rem(ty + dy, d.ty), lax.rem(tx + dx, d.tx)))
    for peer in peers:
        pl.semaphore_signal(barrier, inc=1, device_id=peer, device_id_type=MESH)

    blocks = d.width // LANES
    for i, copy in enumerate(in_tok):
        copy.wait()
        mine = tok_v[i].astype(F32)
        for c in range(blocks):
            pack_v[i, pl.ds(c, d.tok, stride=blocks), :] = mine[:, c * LANES : (c + 1) * LANES]
        gath[i, tx, ty] = pack_v[i].astype(BF16)
    in_grad.wait()
    lane_rows = lax.broadcasted_iota(jnp.int32, (rows, TILE, LANES), 1)
    for side, base, row in ((0, 0, 0), (1, cols - TILE, TILE - 1)):
        edge = grad_v[1 : rows + 1, base : base + TILE, :].astype(F32)
        edge = jnp.sum(jnp.where(lane_rows == row, edge, 0.0), axis=1)
        col_send[side] = edge.astype(BF16)

    pl.semaphore_wait(barrier, len(peers))

    up, down = ty > 0, ty < d.ty - 1
    left, right = tx > 0, tx < d.tx - 1
    upper, lower = lax.rem(ty + d.ty - 1, d.ty), lax.rem(ty + 1, d.ty)
    row_up = send(grad_v.at[1], grad_v.at[rows + 1], "row", 0, 1, at_ty(upper))
    row_down = send(grad_v.at[rows], grad_v.at[0], "row", 1, 0, at_ty(lower))
    start(row_up, up)
    start(row_down, down)
    arrivals = []
    for side, there, out_ok, in_ok in (
        (0, lax.rem(tx + d.tx - 1, d.tx), left, right),
        (1, lax.rem(tx + 1, d.tx), right, left),
    ):
        for dy, there_y, out_y, in_y in (
            (0, upper, up, down),
            (1, ty, True, True),
            (2, lower, down, up),
        ):
            copy = send(
                col_send.at[side],
                col_recv.at[1 - side, 2 - dy],
                "col",
                side * 3 + dy,
                (1 - side) * 3 + 2 - dy,
                (rep, there_y, there),
            )
            start(copy, jnp.logical_and(out_ok, out_y))
            arrivals.append((jnp.logical_and(in_ok, in_y), copy, 1 - side, 2 - dy))

    def tok_z(i):
        return send(
            gath.at[:, tx, ty], gath.at[:, tx, ty], "tok_z", i, i, at_ty(lax.rem(ty + i, d.ty))
        )

    for i in range(1, d.ty):
        start(tok_z(i))

    col_halo[...] = jnp.zeros_like(col_halo)

    @pl.when(jnp.logical_not(up))
    def _():
        grad_v[0] = jnp.zeros((cols, LANES), BF16)

    @pl.when(jnp.logical_not(down))
    def _():
        grad_v[rows + 1] = jnp.zeros((cols, LANES), BF16)

    pl.when(up)(row_down.wait_recv)
    pl.when(down)(row_up.wait_recv)
    for ok, copy, side, place in arrivals:

        @pl.when(ok)
        def _(copy=copy, side=side, place=place):
            copy.wait_recv()
            tile = col_recv[side, place].astype(F32)
            if place == 0:
                col_halo[side, 0:1] = tile[rows - 1 : rows]
            elif place == 1:
                col_halo[side, 1 : rows + 1] = tile
            else:
                col_halo[side, rows + 1 : rows + 2] = tile[0:1]

    for i in range(1, d.ty):
        tok_z(i).wait_recv()

    def tok_t(i):
        return send(gath.at[:, tx], gath.at[:, tx], "tok_t", i, i, at_tx(lax.rem(tx + i, d.tx)))

    for i in range(1, d.tx):
        start(tok_t(i))

    col_index = lax.broadcasted_iota(jnp.int32, (cols, LANES), 0)

    def shift_row(r, carry):
        line = grad_v[r]
        wide_line = line.astype(F32)
        before = jnp.where(col_index == 0, col_halo[0, pl.ds(r, 1)], pltpu.roll(wide_line, 1, 0))
        after = jnp.where(
            col_index == cols - 1, col_halo[1, pl.ds(r, 1)], pltpu.roll(wide_line, cols - 1, 0)
        )
        shifted[r, :, 0:LANES] = after.astype(BF16)
        shifted[r, :, LANES : 2 * LANES] = line
        shifted[r, :, 2 * LANES :] = before.astype(BF16)
        return carry

    lax.fori_loop(0, rows + 2, shift_row, 0)
    in_feat.wait()

    group = 4
    pixels = group * cols

    def neighbours(r):
        return jnp.concatenate(
            [
                shifted[pl.ds(r + 2 - ky, group)].reshape(pixels, 3 * LANES)
                for ky in range(3)
            ],
            axis=-1,
        )

    acc[...] = jnp.zeros_like(acc)

    def weight_step(i, carry):
        value = feat_v[pl.ds(i * group, group)].reshape(pixels, LANES).astype(F32)
        active = (value * jax.nn.sigmoid(value)).astype(BF16)
        acc[...] += dot(active, neighbours(i * group), TN)
        return carry

    lax.fori_loop(0, rows // group, weight_step, 0)
    for k in range(9):
        part_v[k * LANES : (k + 1) * LANES, :] = acc[:, k * LANES : (k + 1) * LANES].astype(BF16)

    def slab(t):
        return pl.ds(pl.multiple_of(t * d.part, TILE), d.part)

    def scatter(i):
        there = lax.rem(tx + i, d.tx)
        return send(part_v.at[slab(there)], scatter_v.at[i], "scatter", i, i, at_tx(there))

    for i in range(1, d.tx):
        start(scatter(i))

    for copy in in_taps:
        copy.wait()

    def feature_step(i, carry):
        here = pl.ds(i * group, group)
        value = feat_v[here].reshape(pixels, LANES).astype(F32)
        gate = jax.nn.sigmoid(value)
        slope = gate * (1.0 + value * (1.0 - gate))
        act_grad = dot(neighbours(i * group), taps[...], NT)
        upstream = grad_v[pl.ds(i * group + 1, group)].reshape(pixels, LANES).astype(F32)
        out_v[here] = (upstream + slope * act_grad).astype(BF16).reshape(group, cols, LANES)
        return carry

    lax.fori_loop(0, rows // group, feature_step, 0)
    out_feature = local(out_v, feature_out.at[0], 16)

    for i in range(1, d.tx):
        scatter(i).wait_recv()
    total = part_v[slab(tx)].astype(F32)
    for i in range(1, d.tx):
        total = total + scatter_v[i].astype(F32)
    sum_v[x] = total.astype(BF16)

    def sum_x(i):
        return send(sum_v.at[x], sum_v.at[x], "sum_x", i, i, at_x(i))

    for i in range(1, d.x):
        start(sum_x(i))

    for i in range(1, d.tx):
        tok_t(i).wait_recv()
    for i in range(2):
        wide[...] = gath[i].reshape(d.tokens * blocks, LANES).astype(F32)
        for c in range(blocks):
            tok_all[i, :, c * LANES : (c + 1) * LANES] = wide[
                pl.ds(c, d.tokens, stride=blocks), :
            ].astype(BF16)
    for i, copy in enumerate(in_proj):
        copy.wait()
        qkv[:, i * d.width : (i + 1) * d.width] = dot(tok_all[0], proj_w[i], NN).astype(BF16)

    for i in range(1, d.x):
        sum_x(i).wait_recv()
    total = sum_v[0].astype(F32)
    for i in range(1, d.x):
        total = total + sum_v[i].astype(F32)
    total_v[...] = total.astype(BF16)

    def own(j):
        return send(
            total_v.at[pl.ds(j * d.piece, d.piece)],
            own_v.at[z],
            "own",
            j,
            z,
            at_z(d.owner(j)),
        )

    def own_from(k):
        return send(total_v.at[pl.ds(0, d.piece)], own_v.at[k], "own", 0, k, at_z(k))

    for j in range(d.owners):
        start(own(j), z != d.owner(j))

    lane = lax.broadcasted_iota(jnp.int32, (d.tokens, LANES), 1)
    low = lane < HEAD_DIM
    scale = 1.0 / HEAD_DIM**0.5

    def head_pair(p, carry):
        def block(ref, offset):
            return ref[:, pl.ds(pl.multiple_of(offset + p * LANES, LANES), LANES)]

        def halves(v):
            zero = jnp.zeros_like(v)
            return jnp.concatenate([jnp.where(low, v, zero), jnp.where(low, zero, v)], axis=0)

        key = block(qkv, d.width)
        value = block(qkv, 2 * d.width)
        query2 = halves(block(qkv, 0))
        upstream2 = halves(block(tok_all.at[1], 0))
        scores = dot(key, query2, NT) * scale
        expos = jnp.exp(scores - jnp.max(scores, axis=0, keepdims=True))
        probs = expos / jnp.sum(expos, axis=0, keepdims=True)
        dprobs = dot(value, upstream2, NT)
        dscores = probs * (dprobs - jnp.sum(dprobs * probs, axis=0, keepdims=True))
        dscores_low = (dscores * scale).astype(BF16)
        value_grad = dot(probs.astype(BF16), upstream2, NN)
        key_grad = dot(dscores_low, query2, NN)
        both = dot(dscores_low, key, TN)
        query_grad = jnp.where(low, both[: d.tokens], both[d.tokens :])
        for i, g in enumerate((query_grad, key_grad, value_grad)):
            here = pl.ds(pl.multiple_of(i * d.width + p * LANES, LANES), LANES)
            pgrad[:, here] = g.astype(BF16)
        return carry

    pairs = d.width // LANES
    lax.fori_loop(0, pairs // 2, head_pair, 0)

    def cast(j, k):
        here = fin.at[tx, pl.ds(j * d.piece, d.piece)]
        return send(here, here, "cast", k, j, at_z(k))

    for j in range(d.owners):

        @pl.when(z == d.owner(j))
        def _(j=j):
            own_v[z] = total_v[j * d.piece : (j + 1) * d.piece]
            for k in range(d.z):
                if k != d.owner(j):
                    own_from(k).wait_recv()
            whole = own_v[0].astype(F32)
            for k in range(1, d.z):
                whole = whole + own_v[k].astype(F32)
            fin[tx, j * d.piece : (j + 1) * d.piece] = whole.astype(BF16)
            for k in range(d.z):
                if k != d.owner(j):
                    cast(j, k).start()

    lax.fori_loop(pairs // 2, pairs, head_pair, 0)

    place = (tx * d.ty + ty) * d.tok
    channels = d.width // (d.ty * d.tx)
    first = (ty * d.tx + tx) * channels
    pick_row = lax.broadcasted_iota(jnp.int32, (2 * 8, d.width), 0)
    pick_col = lax.broadcasted_iota(jnp.int32, (2 * 8, d.width), 1)
    pick = jnp.logical_and(pick_col == first + pick_row, pick_row < 8).astype(F32).astype(BF16)
    columns = dot(pick, tok_all[0], NT)
    own_row = lax.broadcasted_iota(jnp.int32, (2 * 8, d.tokens), 0)
    own_col = lax.broadcasted_iota(jnp.int32, (2 * 8, d.tokens), 1)
    picked = jnp.where(
        own_row < 8, columns, (own_col == place + own_row - 8).astype(F32)
    ).astype(BF16)
    both = dot(picked, pgrad[...], NN)
    half = 3 * d.width // 2
    pz_v[zh] = jnp.concatenate([both[:8, :half], both[:8, half:]], axis=0).astype(BF16)
    proj_z = send(pz_v.at[zh], pz_v.at[zh], "proj_z", 0, 0, at_z(lax.rem(z + d.ty, d.z)))
    start(proj_z)
    own_grads = both[8:].astype(BF16)
    back = jnp.zeros((8, d.width), F32)
    for i in range(3):
        back = back + dot(own_grads[:, i * d.width : (i + 1) * d.width], proj_w[i], NT)
    token_out[0] = (tok_v[1].astype(F32) + back[: d.tok]).astype(BF16)

    for j in range(d.owners):
        pl.when(z != d.owner(j))(cast(j, d.owner(j)).wait_recv)

    def gather(i):
        return send(fin.at[tx], fin.at[tx], "gather", i, i, at_tx(lax.rem(tx + i, d.tx)))

    for i in range(1, d.tx):
        start(gather(i))

    proj_z.wait_recv()
    px_v[x] = (pz_v[0].astype(F32) + pz_v[1].astype(F32)).astype(BF16)

    def proj_x(i):
        return send(px_v.at[x], px_v.at[x], "proj_x", i, i, at_x(i))

    for i in range(1, d.x):
        start(proj_x(i))
    for i in range(1, d.x):
        proj_x(i).wait_recv()
    total = px_v[0].astype(F32)
    for i in range(1, d.x):
        total = total + px_v[i].astype(F32)
    proj_out[:, :half] = total[:8]
    proj_out[:, half:] = total[8:]

    for i in range(1, d.tx):
        gather(i).wait_recv()
    out_weight = local(fin, weight_out, 17)

    for when, copy in sent:
        if when is None:
            copy.wait_send()
        else:
            pl.when(when)(copy.wait_send)
    for j in range(d.owners):

        @pl.when(z == d.owner(j))
        def _(j=j):
            for k in range(d.z):
                if k != d.owner(j):
                    cast(j, k).wait_send()

    out_feature.wait()
    out_weight.wait()


def shards(d, *args):
    tile = (d.rows, d.cols, LANES)
    half = 3 * d.width // 2
    blocks = d.width // LANES
    packed = d.tok * blocks
    assert packed == TILE and d.rows == TILE
    _, messages = message_slots(d)
    hbm = pl.BlockSpec(memory_space=pl.ANY)
    vmem = pl.BlockSpec(memory_space=pltpu.VMEM)
    feature_grad, weight_grad, token_grad, proj_grad = pl.pallas_call(
        functools.partial(kernel, d),
        out_shape=(
            jax.ShapeDtypeStruct((1, *tile), BF16),
            jax.ShapeDtypeStruct((d.tx, d.part, LANES), BF16),
            jax.ShapeDtypeStruct((1, d.tok, d.width), BF16),
            jax.ShapeDtypeStruct((8, 3 * d.width), F32),
        ),
        in_specs=[hbm] * 8,
        out_specs=(hbm, hbm, vmem, vmem),
        scratch_shapes=[
            pltpu.VMEM(tile, BF16),
            pltpu.VMEM((d.rows + 2, d.cols, LANES), BF16),
            pltpu.VMEM((d.rows + 2, d.cols, 3 * LANES), BF16),
            pltpu.VMEM((LANES, 9 * LANES), BF16),
            pltpu.VMEM((3, d.width, d.width), BF16),
            pltpu.VMEM(tile, BF16),
            pltpu.VMEM((LANES, 9 * LANES), F32),
            pltpu.VMEM((9 * LANES, LANES), BF16),
            pltpu.VMEM((d.tx, d.part, LANES), BF16),
            pltpu.VMEM((d.x, d.part, LANES), BF16),
            pltpu.VMEM((d.part, LANES), BF16),
            pltpu.VMEM((d.z, d.piece, LANES), BF16),
            pltpu.VMEM((d.tx, d.part, LANES), BF16),
            pltpu.VMEM((2, d.rows, LANES), BF16),
            pltpu.VMEM((2, 3, d.rows, LANES), BF16),
            pltpu.VMEM((2, d.rows + 8, LANES), F32),
            pltpu.VMEM((2, d.tok, d.width), BF16),
            pltpu.VMEM((2, packed, LANES), F32),
            pltpu.VMEM((2, d.tx, d.ty, packed, LANES), BF16),
            pltpu.VMEM((d.tokens * blocks, LANES), F32),
            pltpu.VMEM((2, d.tokens, d.width), BF16),
            pltpu.VMEM((d.tokens, 3 * d.width), BF16),
            pltpu.VMEM((d.tokens, 3 * d.width), BF16),
            pltpu.VMEM((d.zh, 16, half), BF16),
            pltpu.VMEM((d.x, 16, half), BF16),
            pltpu.SemaphoreType.DMA((18,)),
            pltpu.SemaphoreType.DMA((messages,)),
            pltpu.SemaphoreType.DMA((messages,)),
        ],
        compiler_params=pltpu.CompilerParams(
            collective_id=0, has_side_effects=True, vmem_limit_bytes=48 * 1024 * 1024
        ),
    )(*args)
    conv_weight_grad = weight_grad.astype(F32).reshape(3, 3, LANES, LANES)
    return feature_grad, conv_weight_grad, token_grad, proj_grad


def solution(mesh):
    sizes = mesh.shape
    zh = 2

    def whole(*args):
        _, height, width, _ = args[0].shape
        _, tokens, channels = args[3].shape
        d = Dims(
            x=sizes["rep"] // zh,
            zh=zh,
            ty=sizes["ty"],
            tx=sizes["tx"],
            rows=height // sizes["ty"],
            cols=width // sizes["tx"],
            tok=tokens // (sizes["ty"] * sizes["tx"]),
            width=channels,
        )
        in_specs = (
            P("rep", "ty", "tx", None),
            P("rep", "ty", "tx", None),
            P(),
            P("rep", ("ty", "tx"), None),
            P("rep", ("ty", "tx"), None),
            P(),
            P(),
            P(),
        )
        out_specs = (
            P("rep", "ty", "tx", None),
            P(),
            P("rep", ("ty", "tx"), None),
            P(("ty", "tx"), None),
        )
        return jax.shard_map(
            functools.partial(shards, d),
            mesh=mesh,
            in_specs=in_specs,
            out_specs=out_specs,
            check_vma=False,
        )(*args)

    return whole
```

```python
import dataclasses
import functools

import jax
import jax.numpy as jnp
from jax import lax
from jax.experimental import pallas as pl
from jax.experimental.pallas import tpu as pltpu
from jax.sharding import PartitionSpec as P

HEAD_DIM = 64
LANES = 128
TILE = 16
CORES = 2
VMEM_LIMIT = 60 * 1024 * 1024
MESH = pl.DeviceIdType.MESH
BF16 = jnp.bfloat16
F32 = jnp.float32

NN = (((1,), (0,)), ((), ()))
NT = (((1,), (1,)), ((), ()))
TN = (((0,), (0,)), ((), ()))


def dot(a, b, dims):
    return lax.dot_general(a, b, dims, preferred_element_type=F32)


@dataclasses.dataclass(frozen=True)
class Dims:
    x: int
    zh: int
    ty: int
    y: int
    rows: int
    cols: int
    tok: int
    width: int

    @property
    def z(self):
        return self.zh * self.ty

    @property
    def tx(self):
        return self.y * CORES

    @property
    def chips(self):
        return self.x * self.y

    @property
    def half(self):
        return 9 * LANES // CORES

    @property
    def owners(self):
        return 12 if self.chips > 12 else self.chips - 1

    @property
    def piece(self):
        return self.half // self.owners

    @property
    def tokens(self):
        return self.ty * self.tx * self.tok


def message_slots(d):
    slots = {}
    count = 0
    for name, n in (
        ("row", 2),
        ("col", 6),
        ("tok_z", d.ty),
        ("tok_y", d.y),
        ("tok_core", 1),
        ("core", 1),
        ("plane", d.chips),
        ("along_z", d.z),
        ("spread", d.chips),
        ("core_back", 1),
        ("proj_z", 1),
        ("proj_x", d.x),
    ):
        slots[name] = count
        count += n
    return slots, count


def kernel(
    d,
    features,
    fine_grad,
    conv_weight,
    bottom,
    bottom_grad,
    query_weight,
    key_weight,
    value_weight,
    feature_out,
    weight_out,
    token_out,
    proj_out,
    feat_v,
    grad_v,
    shifted,
    taps,
    proj_w,
    out_v,
    acc,
    flat,
    core_send,
    core_v,
    half_v,
    plane_v,
    z_v,
    fin,
    col_send,
    col_recv,
    col_halo,
    tok_v,
    pack_v,
    gath,
    wide,
    tok_all,
    qkv,
    pgrad,
    pz_v,
    px_v,
    local_sem,
    send_sem,
    recv_sem,
):
    slots, _ = message_slots(d)
    rows, cols = d.rows, d.cols
    rep, ty, tx = (lax.axis_index(a) for a in ("rep", "ty", "tx"))
    x, zh = rep // d.zh, rep % d.zh
    y, core = tx // CORES, tx % CORES
    z = zh * d.ty + ty
    chip = y * d.x + x

    def at_chip(c):
        return (lax.rem(c, d.x) * d.zh + zh, ty, (c // d.x) * CORES + core)

    def at_z(k):
        return (x * d.zh + k // d.ty, lax.rem(k, d.ty), tx)

    def at_tx(t):
        return (rep, ty, t)

    def at_ty(t):
        return (rep, t, tx)

    other_core = at_tx(y * CORES + 1 - core)

    def send(src, dst, name, out_index, in_index, device):
        return pltpu.make_async_remote_copy(
            src_ref=src,
            dst_ref=dst,
            send_sem=send_sem.at[slots[name] + out_index],
            recv_sem=recv_sem.at[slots[name] + in_index],
            device_id=device,
            device_id_type=MESH,
        )

    sent = []

    def start(copy, when=None):
        sent.append((when, copy))
        if when is None:
            copy.start()
        else:
            pl.when(when)(copy.start)

    def local(src, dst, i):
        copy = pltpu.make_async_copy(src, dst, local_sem.at[i])
        copy.start()
        return copy

    in_tok = [local(bottom.at[0], tok_v.at[0], 0), local(bottom_grad.at[0], tok_v.at[1], 1)]
    in_grad = local(fine_grad.at[0], grad_v.at[pl.ds(1, rows)], 2)
    in_feat = local(features.at[0], feat_v, 3)

    barrier = pltpu.get_barrier_semaphore()
    peers = [other_core]
    peers += [at_tx(lax.rem(tx + i, d.tx)) for i in (1, d.tx - 1)]
    peers += [at_chip(lax.rem(chip + i, d.chips)) for i in range(1, d.chips)]
    peers += [at_z(lax.rem(z + i, d.z)) for i in range(1, d.z)]
    for dy in (1, d.ty - 1):
        for dx in (1, d.tx - 1):
            peers.append((rep, lax.rem(ty + dy, d.ty), lax.rem(tx + dx, d.tx)))
    for peer in peers:
        pl.semaphore_signal(barrier, inc=1, device_id=peer, device_id_type=MESH)

    in_taps = [
        local(conv_weight.at[k // 3, k % 3], taps.at[:, pl.ds(k * LANES, LANES)], 7 + k)
        for k in range(9)
    ]
    in_proj = [
        local(w, proj_w.at[i], 4 + i) for i, w in enumerate((query_weight, key_weight, value_weight))
    ]

    blocks = d.width // LANES
    for i, copy in enumerate(in_tok):
        copy.wait()
        mine = tok_v[i].astype(F32)
        for c in range(blocks):
            pack_v[i, pl.ds(c, d.tok, stride=blocks), :] = mine[:, c * LANES : (c + 1) * LANES]
        gath[core, i, y, ty] = pack_v[i].astype(BF16)
    in_grad.wait()
    lane_rows = lax.broadcasted_iota(jnp.int32, (rows, TILE, LANES), 1)

    def column(ref, first, side):
        base, row = ((0, 0), (cols - TILE, TILE - 1))[side]
        edge = ref[first : first + rows, base : base + TILE, :].astype(F32)
        return jnp.sum(jnp.where(lane_rows == row, edge, 0.0), axis=1)

    for side in range(2):
        col_send[side] = column(grad_v, 1, side).astype(BF16)

    pl.semaphore_wait(barrier, len(peers))

    up, down = ty > 0, ty < d.ty - 1
    left, right = tx > 0, tx < d.tx - 1
    upper, lower = lax.rem(ty + d.ty - 1, d.ty), lax.rem(ty + 1, d.ty)
    row_up = send(grad_v.at[1], grad_v.at[rows + 1], "row", 0, 1, at_ty(upper))
    row_down = send(grad_v.at[rows], grad_v.at[0], "row", 1, 0, at_ty(lower))
    start(row_up, up)
    start(row_down, down)
    arrivals = []
    for side, there, out_ok, in_ok in (
        (0, lax.rem(tx + d.tx - 1, d.tx), left, right),
        (1, lax.rem(tx + 1, d.tx), right, left),
    ):
        for dy, there_y, out_y, in_y in (
            (0, upper, up, down),
            (1, ty, True, True),
            (2, lower, down, up),
        ):
            copy = send(
                col_send.at[side],
                col_recv.at[1 - side, 2 - dy],
                "col",
                side * 3 + dy,
                (1 - side) * 3 + 2 - dy,
                (rep, there_y, there),
            )
            start(copy, jnp.logical_and(out_ok, out_y))
            arrivals.append((jnp.logical_and(in_ok, in_y), copy, 1 - side, 2 - dy))

    def tok_z(i):
        mine = gath.at[core, :, y, ty]
        return send(mine, mine, "tok_z", i, i, at_ty(lax.rem(ty + i, d.ty)))

    for i in range(1, d.ty):
        start(tok_z(i))

    col_halo[...] = jnp.zeros_like(col_halo)
    col_index = lax.broadcasted_iota(jnp.int32, (cols, LANES), 0)

    def shift_row(r, carry):
        line = grad_v[r]
        wide_line = line.astype(F32)
        before = jnp.where(col_index == 0, col_halo[0, pl.ds(r, 1)], pltpu.roll(wide_line, 1, 0))
        after = jnp.where(
            col_index == cols - 1, col_halo[1, pl.ds(r, 1)], pltpu.roll(wide_line, cols - 1, 0)
        )
        shifted[r, :, 0:LANES] = after.astype(BF16)
        shifted[r, :, LANES : 2 * LANES] = line
        shifted[r, :, 2 * LANES :] = before.astype(BF16)
        return carry

    lax.fori_loop(1, rows + 1, shift_row, 0)
    for r in (0, rows + 1):
        shifted[r] = jnp.zeros((cols, 3 * LANES), BF16)
    in_feat.wait()

    group = 4
    pixels = group * cols

    def neighbours(r):
        return jnp.concatenate(
            [
                shifted[pl.ds(r + 2 - ky, group)].reshape(pixels, 3 * LANES)
                for ky in range(3)
            ],
            axis=-1,
        )

    def silu(v):
        value = v.astype(F32)
        return (value * jax.nn.sigmoid(value)).astype(BF16)

    acc[...] = jnp.zeros_like(acc)

    def weight_step(i, carry):
        active = silu(feat_v[pl.ds(i * group, group)].reshape(pixels, LANES))
        acc[...] += dot(active, neighbours(i * group), TN)
        return carry

    lax.fori_loop(0, rows // group, weight_step, 0)

    @pl.when(jnp.logical_not(up))
    def _():
        grad_v[0] = jnp.zeros((cols, LANES), BF16)

    @pl.when(jnp.logical_not(down))
    def _():
        grad_v[rows + 1] = jnp.zeros((cols, LANES), BF16)

    pl.when(up)(row_down.wait_recv)
    pl.when(down)(row_up.wait_recv)
    for ok, copy, side, place in arrivals:

        @pl.when(ok)
        def _(copy=copy, side=side, place=place):
            copy.wait_recv()
            tile = col_recv[side, place].astype(F32)
            if place == 0:
                col_halo[side, 0:1] = tile[rows - 1 : rows]
            elif place == 1:
                col_halo[side, 1 : rows + 1] = tile
            else:
                col_halo[side, rows + 1 : rows + 2] = tile[0:1]

    for r, inner, ky in ((0, 0, 2), (rows + 1, rows - 1, 0)):
        shift_row(r, 0)
        acc[:, ky * 3 * LANES : (ky + 1) * 3 * LANES] += dot(silu(feat_v[inner]), shifted[r], TN)
    halo_row = lax.broadcasted_iota(jnp.int32, (rows + 8, LANES), 0)
    inside = jnp.logical_and(halo_row >= 1, halo_row <= rows)
    for side, kx in ((0, 2), (1, 0)):
        active = silu(column(feat_v, 0, side))
        line = jnp.where(inside, col_halo[side], 0.0)
        three = jnp.concatenate([line[2 - ky : 2 - ky + rows] for ky in range(3)], axis=1)
        more = dot(active, three.astype(BF16), TN)
        for ky in range(3):
            k = ky * 3 + kx
            acc[:, k * LANES : (k + 1) * LANES] += more[:, ky * LANES : (ky + 1) * LANES]
    for k in range(9):
        flat[k * LANES : (k + 1) * LANES, :] = acc[:, k * LANES : (k + 1) * LANES]

    def core_rows(c):
        return pl.ds(pl.multiple_of(c * d.half, TILE), d.half)

    core_send[...] = flat[core_rows(1 - core), :].astype(BF16)
    to_core = send(core_send, core_v, "core", 0, 0, other_core)
    start(to_core)

    tile_row = lax.broadcasted_iota(jnp.int32, (TILE, LANES), 0)

    def fix_row(r, carry):
        for side, base, lanes, row in ((0, 0, 2 * LANES, 0), (1, cols - TILE, 0, TILE - 1)):
            here = (r, pl.ds(base, TILE), pl.ds(lanes, LANES))
            tile = shifted[here].astype(F32)
            tile = jnp.where(tile_row == row, col_halo[side, pl.ds(r, 1)], tile)
            shifted[here] = tile.astype(BF16)
        return carry

    lax.fori_loop(1, rows + 1, fix_row, 0)

    to_core.wait_recv()
    half_v[...] = (flat[core_rows(core), :] + core_v[...].astype(F32)).astype(BF16)
    first = core * (d.chips - d.owners)
    piece = chip - first
    owner = jnp.logical_and(piece >= 0, piece < d.owners)

    def to_plane(p):
        return send(
            half_v.at[pl.ds(p * d.piece, d.piece)],
            plane_v.at[chip],
            "plane",
            p,
            chip,
            at_chip(first + p),
        )

    def from_plane(i):
        there = lax.rem(chip + i, d.chips)
        return send(half_v.at[pl.ds(0, d.piece)], plane_v.at[there], "plane", 0, there, at_chip(there))

    for p in range(d.owners):
        start(to_plane(p), piece != p)

    for i in range(1, d.ty):
        tok_z(i).wait_recv()

    def tok_y(i):
        mine = gath.at[core, :, y]
        return send(mine, mine, "tok_y", i, i, at_tx(lax.rem(tx + i * CORES, d.tx)))

    for i in range(1, d.y):
        start(tok_y(i))

    for copy in in_taps:
        copy.wait()

    def feature_step(i, carry):
        here = pl.ds(i * group, group)
        value = feat_v[here].reshape(pixels, LANES).astype(F32)
        gate = jax.nn.sigmoid(value)
        slope = gate * (1.0 + value * (1.0 - gate))
        act_grad = dot(neighbours(i * group), taps[...], NT)
        upstream = grad_v[pl.ds(i * group + 1, group)].reshape(pixels, LANES).astype(F32)
        out_v[here] = (upstream + slope * act_grad).astype(BF16).reshape(group, cols, LANES)
        return carry

    lax.fori_loop(0, rows // group, feature_step, 0)
    out_feature = local(out_v, feature_out.at[0], 16)

    def along_z(i):
        return send(z_v.at[z], z_v.at[z], "along_z", i, i, at_z(lax.rem(z + i, d.z)))

    @pl.when(owner)
    def _():
        here = pl.ds(pl.multiple_of(piece * d.piece, TILE), d.piece)
        plane_v[chip] = half_v[here, :]
        for i in range(1, d.chips):
            from_plane(i).wait_recv()
        total = plane_v[0].astype(F32)
        for i in range(1, d.chips):
            total = total + plane_v[i].astype(F32)
        z_v[z] = total.astype(BF16)
        for i in range(1, d.z):
            along_z(i).start()

    for i in range(1, d.y):
        tok_y(i).wait_recv()
    to_core_tok = send(gath.at[core], gath.at[core], "tok_core", 0, 0, other_core)
    start(to_core_tok)
    to_core_tok.wait_recv()

    share = d.tokens // CORES
    for c in range(CORES):
        for i in range(2):
            wide[...] = gath[c, i].reshape(share * blocks, LANES).astype(F32)
            for b in range(blocks):
                tok_all[i, c * share : (c + 1) * share, b * LANES : (b + 1) * LANES] = wide[
                    pl.ds(b, share, stride=blocks), :
                ].astype(BF16)
    for i, copy in enumerate(in_proj):
        copy.wait()
        qkv[:, i * d.width : (i + 1) * d.width] = dot(tok_all[0], proj_w[i], NN).astype(BF16)

    lane = lax.broadcasted_iota(jnp.int32, (d.tokens, LANES), 1)
    low = lane < HEAD_DIM
    scale = 1.0 / HEAD_DIM**0.5

    def head_pair(p, carry):
        def block(ref, offset):
            return ref[:, pl.ds(pl.multiple_of(offset + p * LANES, LANES), LANES)]

        def halves(v):
            zero = jnp.zeros_like(v)
            return jnp.concatenate([jnp.where(low, v, zero), jnp.where(low, zero, v)], axis=0)

        key = block(qkv, d.width)
        value = block(qkv, 2 * d.width)
        query2 = halves(block(qkv, 0))
        upstream2 = halves(block(tok_all.at[1], 0))
        scores = dot(key, query2, NT) * scale
        expos = jnp.exp(scores - jnp.max(scores, axis=0, keepdims=True))
        probs = expos / jnp.sum(expos, axis=0, keepdims=True)
        dprobs = dot(value, upstream2, NT)
        dscores = probs * (dprobs - jnp.sum(dprobs * probs, axis=0, keepdims=True))
        dscores_low = (dscores * scale).astype(BF16)
        value_grad = dot(probs.astype(BF16), upstream2, NN)
        key_grad = dot(dscores_low, query2, NN)
        both = dot(dscores_low, key, TN)
        query_grad = jnp.where(low, both[: d.tokens], both[d.tokens :])
        for i, g in enumerate((query_grad, key_grad, value_grad)):
            here = pl.ds(pl.multiple_of(i * d.width + p * LANES, LANES), LANES)
            pgrad[:, here] = g.astype(BF16)
        return carry

    lax.fori_loop(0, d.width // LANES, head_pair, 0)

    place = ((core * d.y + y) * d.ty + ty) * d.tok
    channel = (ty * d.tx + tx) * (d.width // (d.ty * d.tx))
    pick_row = lax.broadcasted_iota(jnp.int32, (2 * 8, d.width), 0)
    pick_col = lax.broadcasted_iota(jnp.int32, (2 * 8, d.width), 1)
    pick = jnp.logical_and(pick_col == channel + pick_row, pick_row < 8).astype(F32).astype(BF16)
    columns = dot(pick, tok_all[0], NT)
    own_row = lax.broadcasted_iota(jnp.int32, (2 * 8, d.tokens), 0)
    own_col = lax.broadcasted_iota(jnp.int32, (2 * 8, d.tokens), 1)
    picked = jnp.where(
        own_row < 8, columns, (own_col == place + own_row - 8).astype(F32)
    ).astype(BF16)
    both = dot(picked, pgrad[...], NN)
    half = 3 * d.width // 2
    pz_v[zh] = jnp.concatenate([both[:8, :half], both[:8, half:]], axis=0).astype(BF16)
    proj_z = send(pz_v.at[zh], pz_v.at[zh], "proj_z", 0, 0, at_z(lax.rem(z + d.ty, d.z)))
    start(proj_z)
    own_grads = both[8:].astype(BF16)
    back = jnp.zeros((8, d.width), F32)
    for i in range(3):
        back = back + dot(own_grads[:, i * d.width : (i + 1) * d.width], proj_w[i], NT)
    token_out[0] = (tok_v[1].astype(F32) + back[: d.tok]).astype(BF16)

    def spread(p, i):
        here = fin.at[core, pl.ds(pl.multiple_of(p * d.piece, TILE), d.piece)]
        return send(here, here, "spread", i, p, at_chip(lax.rem(chip + i, d.chips)))

    @pl.when(owner)
    def _():
        for i in range(1, d.z):
            along_z(i).wait_recv()
        total = z_v[0].astype(F32)
        for i in range(1, d.z):
            total = total + z_v[i].astype(F32)
        fin[core, pl.ds(pl.multiple_of(piece * d.piece, TILE), d.piece)] = total.astype(BF16)
        for i in range(1, d.chips):
            spread(piece, i).start()

    proj_z.wait_recv()
    px_v[x] = (pz_v[0].astype(F32) + pz_v[1].astype(F32)).astype(BF16)

    def proj_x(i):
        return send(
            px_v.at[x], px_v.at[x], "proj_x", i, i, (lax.rem(x + i, d.x) * d.zh + zh, ty, tx)
        )

    for i in range(1, d.x):
        start(proj_x(i))

    for p in range(d.owners):
        pl.when(piece != p)(spread(p, 0).wait_recv)
    back_core = send(fin.at[core], fin.at[core], "core_back", 0, 0, other_core)
    start(back_core)

    for i in range(1, d.x):
        proj_x(i).wait_recv()
    total = px_v[0].astype(F32)
    for i in range(1, d.x):
        total = total + px_v[i].astype(F32)
    proj_out[:, :half] = total[:8]
    proj_out[:, half:] = total[8:]

    back_core.wait_recv()
    out_weight = local(fin, weight_out, 17)

    for when, copy in sent:
        if when is None:
            copy.wait_send()
        else:
            pl.when(when)(copy.wait_send)

    @pl.when(owner)
    def _():
        for i in range(1, d.z):
            along_z(i).wait_send()
        for i in range(1, d.chips):
            spread(piece, i).wait_send()

    out_feature.wait()
    out_weight.wait()


def outputs(d, feature, weight, token, proj, feature_out, weight_out, token_out, proj_out, low, high, sem):
    copies = [
        pltpu.make_async_copy(src, dst, sem.at[i])
        for i, (src, dst) in enumerate(
            ((weight, low), (feature, feature_out), (token, token_out), (proj, proj_out))
        )
    ]
    for copy in copies:
        copy.start()
    copies[0].wait()
    high[...] = low[...].astype(F32)
    copies[0] = pltpu.make_async_copy(high, weight_out, sem.at[0])
    copies[0].start()
    for copy in copies:
        copy.wait()


def shards(d, *args):
    tile = (d.rows, d.cols, LANES)
    half = 3 * d.width // 2
    blocks = d.width // LANES
    packed = d.tok * blocks
    assert packed == TILE and d.rows == TILE
    _, messages = message_slots(d)
    hbm = pl.BlockSpec(memory_space=pl.ANY)
    vmem = pl.BlockSpec(memory_space=pltpu.VMEM)
    results = pl.pallas_call(
        functools.partial(kernel, d),
        out_shape=(
            jax.ShapeDtypeStruct((1, *tile), BF16),
            jax.ShapeDtypeStruct((CORES, d.half, LANES), BF16),
            jax.ShapeDtypeStruct((1, d.tok, d.width), BF16),
            jax.ShapeDtypeStruct((8, 3 * d.width), F32),
        ),
        in_specs=[hbm] * 8,
        out_specs=(hbm, hbm, vmem, vmem),
        scratch_shapes=[
            pltpu.VMEM(tile, BF16),
            pltpu.VMEM((d.rows + 2, d.cols, LANES), BF16),
            pltpu.VMEM((d.rows + 2, d.cols, 3 * LANES), BF16),
            pltpu.VMEM((LANES, 9 * LANES), BF16),
            pltpu.VMEM((3, d.width, d.width), BF16),
            pltpu.VMEM(tile, BF16),
            pltpu.VMEM((LANES, 9 * LANES), F32),
            pltpu.VMEM((9 * LANES, LANES), F32),
            pltpu.VMEM((d.half, LANES), BF16),
            pltpu.VMEM((d.half, LANES), BF16),
            pltpu.VMEM((d.half, LANES), BF16),
            pltpu.VMEM((d.chips, d.piece, LANES), BF16),
            pltpu.VMEM((d.z, d.piece, LANES), BF16),
            pltpu.VMEM((CORES, d.half, LANES), BF16),
            pltpu.VMEM((2, d.rows, LANES), BF16),
            pltpu.VMEM((2, 3, d.rows, LANES), BF16),
            pltpu.VMEM((2, d.rows + 8, LANES), F32),
            pltpu.VMEM((2, d.tok, d.width), BF16),
            pltpu.VMEM((2, packed, LANES), F32),
            pltpu.VMEM((CORES, 2, d.y, d.ty, packed, LANES), BF16),
            pltpu.VMEM((d.tokens * blocks // CORES, LANES), F32),
            pltpu.VMEM((2, d.tokens, d.width), BF16),
            pltpu.VMEM((d.tokens, 3 * d.width), BF16),
            pltpu.VMEM((d.tokens, 3 * d.width), BF16),
            pltpu.VMEM((d.zh, 16, half), BF16),
            pltpu.VMEM((d.x, 16, half), BF16),
            pltpu.SemaphoreType.DMA((18,)),
            pltpu.SemaphoreType.DMA((messages,)),
            pltpu.SemaphoreType.DMA((messages,)),
        ],
        compiler_params=pltpu.CompilerParams(
            collective_id=0, has_side_effects=True, vmem_limit_bytes=VMEM_LIMIT
        ),
    )(*args)
    feature_grad, conv_weight_grad, token_grad, proj_grad = pl.pallas_call(
        functools.partial(outputs, d),
        out_shape=(
            jax.ShapeDtypeStruct((1, *tile), BF16),
            jax.ShapeDtypeStruct((CORES, d.half, LANES), F32),
            jax.ShapeDtypeStruct((1, d.tok, d.width), BF16),
            jax.ShapeDtypeStruct((8, 3 * d.width), F32),
        ),
        in_specs=[hbm] * 4,
        out_specs=(hbm,) * 4,
        scratch_shapes=[
            pltpu.VMEM((CORES, d.half, LANES), BF16),
            pltpu.VMEM((CORES, d.half, LANES), F32),
            pltpu.SemaphoreType.DMA((4,)),
        ],
        compiler_params=pltpu.CompilerParams(vmem_limit_bytes=VMEM_LIMIT),
    )(*results)
    return feature_grad, conv_weight_grad.reshape(3, 3, LANES, LANES), token_grad, proj_grad


def solution(mesh):
    sizes = mesh.shape
    zh = 2

    def whole(*args):
        _, height, width, _ = args[0].shape
        _, tokens, channels = args[3].shape
        d = Dims(
            x=sizes["rep"] // zh,
            zh=zh,
            ty=sizes["ty"],
            y=sizes["tx"] // CORES,
            rows=height // sizes["ty"],
            cols=width // sizes["tx"],
            tok=tokens // (sizes["ty"] * sizes["tx"]),
            width=channels,
        )
        in_specs = (
            P("rep", "ty", "tx", None),
            P("rep", "ty", "tx", None),
            P(),
            P("rep", ("ty", "tx"), None),
            P("rep", ("ty", "tx"), None),
            P(),
            P(),
            P(),
        )
        out_specs = (
            P("rep", "ty", "tx", None),
            P(),
            P("rep", ("ty", "tx"), None),
            P(("ty", "tx"), None),
        )
        return jax.shard_map(
            functools.partial(shards, d),
            mesh=mesh,
            in_specs=in_specs,
            out_specs=out_specs,
            check_vma=False,
        )(*args)

    return whole
```

```python
import dataclasses
import functools

import jax
import jax.numpy as jnp
from jax import lax
from jax.experimental import pallas as pl
from jax.experimental.pallas import tpu as pltpu
from jax.sharding import PartitionSpec as P

HEAD_DIM = 64
LANES = 128
TILE = 16
CORES = 2
OUT_PARTS = 4
EARLY = 1
VMEM_LIMIT = 60 * 1024 * 1024
MESH = pl.DeviceIdType.MESH
BF16 = jnp.bfloat16
F32 = jnp.float32

NN = (((1,), (0,)), ((), ()))
NT = (((1,), (1,)), ((), ()))
TN = (((0,), (0,)), ((), ()))


def dot(a, b, dims):
    return lax.dot_general(a, b, dims, preferred_element_type=F32)


@dataclasses.dataclass(frozen=True)
class Dims:
    x: int
    zh: int
    ty: int
    y: int
    rows: int
    cols: int
    tok: int
    width: int

    @property
    def z(self):
        return self.zh * self.ty

    @property
    def tx(self):
        return self.y * CORES

    @property
    def chips(self):
        return self.x * self.y

    @property
    def half(self):
        return 9 * LANES // CORES

    @property
    def piece(self):
        return (self.half // TILE - 1) // self.chips * TILE

    @property
    def extra(self):
        return self.half // TILE - self.chips * (self.piece // TILE)

    @property
    def tokens(self):
        return self.ty * self.tx * self.tok


def message_slots(d):
    slots = {}
    count = 0
    for name, n in (
        ("row", 2),
        ("col", 6),
        ("tok_z", d.ty),
        ("tok_y", d.y * d.ty),
        ("tok_core", 1),
        ("core", 1),
        ("plane", d.chips),
        ("along_z", d.z),
        ("spread", d.chips),
        ("plane_extra", d.chips),
        ("along_z_extra", d.z),
        ("spread_extra", d.chips),
        ("core_back", 1),
        ("proj_z", 1),
        ("proj_x", d.x),
    ):
        slots[name] = count
        count += n
    return slots, count


def kernel(
    d,
    features,
    fine_grad,
    conv_weight,
    bottom,
    bottom_grad,
    query_weight,
    key_weight,
    value_weight,
    feature_out,
    weight_out,
    token_out,
    proj_out,
    feat_v,
    grad_v,
    shifted,
    taps,
    proj_w,
    out_v,
    acc,
    flat,
    core_send,
    core_v,
    half_v,
    plane_v,
    z_v,
    plane_w,
    z_w,
    fin,
    col_send,
    col_recv,
    col_halo,
    tok_v,
    pack_v,
    gath,
    wide,
    tok_all,
    qkv,
    pgrad,
    pz_v,
    px_v,
    local_sem,
    send_sem,
    recv_sem,
):
    slots, _ = message_slots(d)
    rows, cols = d.rows, d.cols
    rep, ty, tx = (lax.axis_index(a) for a in ("rep", "ty", "tx"))
    x, zh = rep // d.zh, rep % d.zh
    y, core = tx // CORES, tx % CORES
    z = zh * d.ty + ty
    chip = y * d.x + x

    def at_chip(c):
        return (lax.rem(c, d.x) * d.zh + zh, ty, (c // d.x) * CORES + core)

    def at_z(k):
        return (x * d.zh + k // d.ty, lax.rem(k, d.ty), tx)

    def at_tx(t):
        return (rep, ty, t)

    def at_ty(t):
        return (rep, t, tx)

    other_core = at_tx(y * CORES + 1 - core)

    def send(src, dst, name, out_index, in_index, device):
        return pltpu.make_async_remote_copy(
            src_ref=src,
            dst_ref=dst,
            send_sem=send_sem.at[slots[name] + out_index],
            recv_sem=recv_sem.at[slots[name] + in_index],
            device_id=device,
            device_id_type=MESH,
        )

    sent = []

    def start(copy, when=None):
        sent.append((when, copy))
        if when is None:
            copy.start()
        else:
            pl.when(when)(copy.start)

    def local(src, dst, i):
        copy = pltpu.make_async_copy(src, dst, local_sem.at[i])
        copy.start()
        return copy

    in_tok = [local(bottom.at[0], tok_v.at[0], 0), local(bottom_grad.at[0], tok_v.at[1], 1)]
    in_grad = local(fine_grad.at[0], grad_v.at[pl.ds(1, rows)], 2)
    in_feat = local(features.at[0], feat_v, 3)

    barrier = pltpu.get_barrier_semaphore()
    peers = [other_core]
    peers += [at_tx(lax.rem(tx + i, d.tx)) for i in (1, d.tx - 1)]
    peers += [at_chip(lax.rem(chip + i, d.chips)) for i in range(1, d.chips)]
    peers += [at_z(lax.rem(z + i, d.z)) for i in range(1, d.z)]
    for dy in (1, d.ty - 1):
        for dx in (1, d.tx - 1):
            peers.append((rep, lax.rem(ty + dy, d.ty), lax.rem(tx + dx, d.tx)))
    for peer in peers:
        pl.semaphore_signal(barrier, inc=1, device_id=peer, device_id_type=MESH)

    in_taps = [
        local(conv_weight.at[k // 3, k % 3], taps.at[:, pl.ds(k * LANES, LANES)], 7 + k)
        for k in range(9)
    ]
    in_proj = [
        local(w, proj_w.at[i], 4 + i) for i, w in enumerate((query_weight, key_weight, value_weight))
    ]

    blocks = d.width // LANES
    for i, copy in enumerate(in_tok):
        copy.wait()
        mine = tok_v[i].astype(F32)
        for c in range(blocks):
            pack_v[i, pl.ds(c, d.tok, stride=blocks), :] = mine[:, c * LANES : (c + 1) * LANES]
        gath[core, i, y, ty] = pack_v[i].astype(BF16)
    in_grad.wait()
    lane_rows = lax.broadcasted_iota(jnp.int32, (rows, TILE, LANES), 1)

    def column(ref, first, side):
        base, row = ((0, 0), (cols - TILE, TILE - 1))[side]
        edge = ref[first : first + rows, base : base + TILE, :].astype(F32)
        return jnp.sum(jnp.where(lane_rows == row, edge, 0.0), axis=1)

    for side in range(2):
        col_send[side] = column(grad_v, 1, side).astype(BF16)

    col_halo[...] = jnp.zeros_like(col_halo)
    col_index = lax.broadcasted_iota(jnp.int32, (cols, LANES), 0)

    def shift_row(r, carry):
        line = grad_v[r]
        wide_line = line.astype(F32)
        before = jnp.where(col_index == 0, col_halo[0, pl.ds(r, 1)], pltpu.roll(wide_line, 1, 0))
        after = jnp.where(
            col_index == cols - 1, col_halo[1, pl.ds(r, 1)], pltpu.roll(wide_line, cols - 1, 0)
        )
        shifted[r, :, 0:LANES] = after.astype(BF16)
        shifted[r, :, LANES : 2 * LANES] = line
        shifted[r, :, 2 * LANES :] = before.astype(BF16)
        return carry

    lax.fori_loop(1, rows + 1, shift_row, 0)
    for r in (0, rows + 1):
        shifted[r] = jnp.zeros((cols, 3 * LANES), BF16)
    in_feat.wait()

    group = 4
    pixels = group * cols

    def neighbours(r):
        return jnp.concatenate(
            [
                shifted[pl.ds(r + 2 - ky, group)].reshape(pixels, 3 * LANES)
                for ky in range(3)
            ],
            axis=-1,
        )

    def silu(v):
        value = v.astype(F32)
        return (value * jax.nn.sigmoid(value)).astype(BF16)

    acc[...] = jnp.zeros_like(acc)

    def weight_step(i, carry):
        active = silu(feat_v[pl.ds(i * group, group)].reshape(pixels, LANES))
        acc[...] += dot(active, neighbours(i * group), TN)
        return carry

    lax.fori_loop(0, EARLY, weight_step, 0)

    pl.semaphore_wait(barrier, len(peers))

    up, down = ty > 0, ty < d.ty - 1
    left, right = tx > 0, tx < d.tx - 1
    upper, lower = lax.rem(ty + d.ty - 1, d.ty), lax.rem(ty + 1, d.ty)
    row_up = send(grad_v.at[1], grad_v.at[rows + 1], "row", 0, 1, at_ty(upper))
    row_down = send(grad_v.at[rows], grad_v.at[0], "row", 1, 0, at_ty(lower))
    start(row_up, up)
    start(row_down, down)
    arrivals = []
    for side, there, out_ok, in_ok in (
        (0, lax.rem(tx + d.tx - 1, d.tx), left, right),
        (1, lax.rem(tx + 1, d.tx), right, left),
    ):
        for dy, there_y, out_y, in_y in (
            (0, upper, up, down),
            (1, ty, True, True),
            (2, lower, down, up),
        ):
            copy = send(
                col_send.at[side],
                col_recv.at[1 - side, 2 - dy],
                "col",
                side * 3 + dy,
                (1 - side) * 3 + 2 - dy,
                (rep, there_y, there),
            )
            start(copy, jnp.logical_and(out_ok, out_y))
            arrivals.append((jnp.logical_and(in_ok, in_y), copy, 1 - side, 2 - dy))

    def tok_z(i):
        mine = gath.at[core, :, y, ty]
        return send(mine, mine, "tok_z", i, ty, at_ty(lax.rem(ty + i, d.ty)))

    def tok_z_from(t):
        there = gath.at[core, :, y, t]
        return send(there, there, "tok_z", 0, t, at_ty(t))

    def tok_y(i, t):
        tile = gath.at[core, :, y, t]
        k = i * d.ty + t
        return send(tile, tile, "tok_y", k, k, at_tx(lax.rem(tx + i * CORES, d.tx)))

    for i in range(1, d.ty):
        start(tok_z(i))
    for i in range(1, d.y):
        tok_y(i, ty).start()

    lax.fori_loop(EARLY, rows // group, weight_step, 0)

    @pl.when(jnp.logical_not(up))
    def _():
        grad_v[0] = jnp.zeros((cols, LANES), BF16)

    @pl.when(jnp.logical_not(down))
    def _():
        grad_v[rows + 1] = jnp.zeros((cols, LANES), BF16)

    pl.when(up)(row_down.wait_recv)
    pl.when(down)(row_up.wait_recv)
    for ok, copy, side, place in arrivals:

        @pl.when(ok)
        def _(copy=copy, side=side, place=place):
            copy.wait_recv()
            tile = col_recv[side, place].astype(F32)
            if place == 0:
                col_halo[side, 0:1] = tile[rows - 1 : rows]
            elif place == 1:
                col_halo[side, 1 : rows + 1] = tile
            else:
                col_halo[side, rows + 1 : rows + 2] = tile[0:1]

    for r, inner, ky in ((0, 0, 2), (rows + 1, rows - 1, 0)):
        shift_row(r, 0)
        acc[:, ky * 3 * LANES : (ky + 1) * 3 * LANES] += dot(silu(feat_v[inner]), shifted[r], TN)
    halo_row = lax.broadcasted_iota(jnp.int32, (rows + 8, LANES), 0)
    inside = jnp.logical_and(halo_row >= 1, halo_row <= rows)
    for side, kx in ((0, 2), (1, 0)):
        active = silu(column(feat_v, 0, side))
        line = jnp.where(inside, col_halo[side], 0.0)
        three = jnp.concatenate([line[2 - ky : 2 - ky + rows] for ky in range(3)], axis=1)
        more = dot(active, three.astype(BF16), TN)
        for ky in range(3):
            k = ky * 3 + kx
            acc[:, k * LANES : (k + 1) * LANES] += more[:, ky * LANES : (ky + 1) * LANES]
    for k in range(9):
        flat[k * LANES : (k + 1) * LANES, :] = acc[:, k * LANES : (k + 1) * LANES]

    def core_rows(c):
        return pl.ds(pl.multiple_of(c * d.half, TILE), d.half)

    core_send[...] = flat[core_rows(1 - core), :].astype(BF16)
    to_core = send(core_send, core_v, "core", 0, 0, other_core)
    start(to_core)

    tile_row = lax.broadcasted_iota(jnp.int32, (TILE, LANES), 0)

    def fix_row(r, carry):
        for side, base, lanes, row in ((0, 0, 2 * LANES, 0), (1, cols - TILE, 0, TILE - 1)):
            here = (r, pl.ds(base, TILE), pl.ds(lanes, LANES))
            tile = shifted[here].astype(F32)
            tile = jnp.where(tile_row == row, col_halo[side, pl.ds(r, 1)], tile)
            shifted[here] = tile.astype(BF16)
        return carry

    lax.fori_loop(1, rows + 1, fix_row, 0)

    to_core.wait_recv()
    half_v[...] = (flat[core_rows(core), :] + core_v[...].astype(F32)).astype(BF16)

    spare = lax.rem(chip + core * (d.chips - d.extra), d.chips)
    has_extra = spare < d.extra
    last = d.chips * d.piece

    def turned(e):
        return lax.rem(e + core * d.extra, d.chips)

    def rows_of(c):
        return pl.ds(pl.multiple_of(c * d.piece, TILE), d.piece)

    def tile_of(e):
        return pl.ds(pl.multiple_of(last + e * TILE, TILE), TILE)

    def to_plane(i):
        there = lax.rem(chip + i, d.chips)
        return send(
            half_v.at[rows_of(there)], plane_v.at[chip], "plane", i, chip, at_chip(there)
        )

    def from_plane(i):
        there = lax.rem(chip + i, d.chips)
        return send(
            half_v.at[rows_of(there)], plane_v.at[there], "plane", i, there, at_chip(there)
        )

    def to_plane_extra(e):
        there = turned(e)
        return send(
            half_v.at[tile_of(e)], plane_w.at[chip], "plane_extra", e, chip, at_chip(there)
        )

    def from_plane_extra(i):
        there = lax.rem(chip + i, d.chips)
        return send(
            half_v.at[tile_of(0)], plane_w.at[there], "plane_extra", 0, there, at_chip(there)
        )

    for i in range(1, d.chips):
        start(to_plane(i))
    for e in range(d.extra):
        start(to_plane_extra(e), spare != e)

    for distance in range(1, d.ty):
        for t in (ty + distance, ty - distance):

            @pl.when(jnp.logical_and(t >= 0, t < d.ty))
            def _(t=t):
                tok_z_from(t).wait_recv()
                for i in range(1, d.y):
                    tok_y(i, t).start()

    for copy in in_taps:
        copy.wait()

    def feature_step(i, carry):
        here = pl.ds(i * group, group)
        value = feat_v[here].reshape(pixels, LANES).astype(F32)
        gate = jax.nn.sigmoid(value)
        slope = gate * (1.0 + value * (1.0 - gate))
        act_grad = dot(neighbours(i * group), taps[...], NT)
        upstream = grad_v[pl.ds(i * group + 1, group)].reshape(pixels, LANES).astype(F32)
        out_v[here] = (upstream + slope * act_grad).astype(BF16).reshape(group, cols, LANES)
        return carry

    lax.fori_loop(0, rows // group, feature_step, 0)
    out_feature = local(out_v, feature_out.at[0], 16)

    def along_z(i):
        return send(z_v.at[z], z_v.at[z], "along_z", i, i, at_z(lax.rem(z + i, d.z)))

    def along_z_extra(i):
        return send(z_w.at[z], z_w.at[z], "along_z_extra", i, i, at_z(lax.rem(z + i, d.z)))

    def summed(ref, count):
        total = ref[0].astype(F32)
        for i in range(1, count):
            total = total + ref[i].astype(F32)
        return total.astype(BF16)

    plane_v[chip] = half_v[rows_of(chip), :]
    for i in range(1, d.chips):
        from_plane(i).wait_recv()
    z_v[z] = summed(plane_v, d.chips)
    for i in range(1, d.z):
        start(along_z(i))

    @pl.when(has_extra)
    def _():
        plane_w[chip] = half_v[tile_of(spare), :]
        for i in range(1, d.chips):
            from_plane_extra(i).wait_recv()
        z_w[z] = summed(plane_w, d.chips)
        for i in range(1, d.z):
            along_z_extra(i).start()

    for t in range(d.ty):
        for i in range(1, d.y):
            tok_y(i, t).wait_recv()
    to_core_tok = send(gath.at[core], gath.at[core], "tok_core", 0, 0, other_core)
    start(to_core_tok)

    share = d.tokens // CORES
    for copy in in_proj:
        copy.wait()
    for c in (core, 1 - core):
        here = pl.ds(pl.multiple_of(c * share, TILE), share)
        if c is not core:
            to_core_tok.wait_recv()
        for i in range(2):
            wide[...] = gath[c, i].reshape(share * blocks, LANES).astype(F32)
            for b in range(blocks):
                tok_all[i, here, b * LANES : (b + 1) * LANES] = wide[
                    pl.ds(b, share, stride=blocks), :
                ].astype(BF16)
        for i in range(3):
            qkv[here, i * d.width : (i + 1) * d.width] = dot(
                tok_all[0, here], proj_w[i], NN
            ).astype(BF16)

    lane = lax.broadcasted_iota(jnp.int32, (d.tokens, LANES), 1)
    low = lane < HEAD_DIM
    scale = 1.0 / HEAD_DIM**0.5

    def head_pair(p, carry):
        def block(ref, offset):
            return ref[:, pl.ds(pl.multiple_of(offset + p * LANES, LANES), LANES)]

        def halves(v):
            zero = jnp.zeros_like(v)
            return jnp.concatenate([jnp.where(low, v, zero), jnp.where(low, zero, v)], axis=0)

        key = block(qkv, d.width)
        value = block(qkv, 2 * d.width)
        query2 = halves(block(qkv, 0))
        upstream2 = halves(block(tok_all.at[1], 0))
        scores = dot(key, query2, NT) * scale
        expos = jnp.exp(scores - jnp.max(scores, axis=0, keepdims=True))
        probs = expos / jnp.sum(expos, axis=0, keepdims=True)
        dprobs = dot(value, upstream2, NT)
        dscores = probs * (dprobs - jnp.sum(dprobs * probs, axis=0, keepdims=True))
        dscores_low = (dscores * scale).astype(BF16)
        value_grad = dot(probs.astype(BF16), upstream2, NN)
        key_grad = dot(dscores_low, query2, NN)
        both = dot(dscores_low, key, TN)
        query_grad = jnp.where(low, both[: d.tokens], both[d.tokens :])
        for i, g in enumerate((query_grad, key_grad, value_grad)):
            here = pl.ds(pl.multiple_of(i * d.width + p * LANES, LANES), LANES)
            pgrad[:, here] = g.astype(BF16)
        return carry

    lax.fori_loop(0, d.width // LANES, head_pair, 0)

    place = ((core * d.y + y) * d.ty + ty) * d.tok
    channel = (ty * d.tx + tx) * (d.width // (d.ty * d.tx))
    pick_row = lax.broadcasted_iota(jnp.int32, (2 * 8, d.width), 0)
    pick_col = lax.broadcasted_iota(jnp.int32, (2 * 8, d.width), 1)
    pick = jnp.logical_and(pick_col == channel + pick_row, pick_row < 8).astype(F32).astype(BF16)
    columns = dot(pick, tok_all[0], NT)
    own_row = lax.broadcasted_iota(jnp.int32, (2 * 8, d.tokens), 0)
    own_col = lax.broadcasted_iota(jnp.int32, (2 * 8, d.tokens), 1)
    picked = jnp.where(
        own_row < 8, columns, (own_col == place + own_row - 8).astype(F32)
    ).astype(BF16)
    both = dot(picked, pgrad[...], NN)
    half = 3 * d.width // 2
    pz_v[zh] = jnp.concatenate([both[:8, :half], both[:8, half:]], axis=0).astype(BF16)
    proj_z = send(pz_v.at[zh], pz_v.at[zh], "proj_z", 0, 0, at_z(lax.rem(z + d.ty, d.z)))
    start(proj_z)
    own_grads = both[8:].astype(BF16)
    back = jnp.zeros((8, d.width), F32)
    for i in range(3):
        back = back + dot(own_grads[:, i * d.width : (i + 1) * d.width], proj_w[i], NT)
    token_out[0] = (tok_v[1].astype(F32) + back[: d.tok]).astype(BF16)

    def spread(c, i):
        here = fin.at[core, rows_of(c)]
        return send(here, here, "spread", i, c, at_chip(lax.rem(chip + i, d.chips)))

    def spread_extra(e, i):
        here = fin.at[core, tile_of(e)]
        return send(here, here, "spread_extra", i, e, at_chip(lax.rem(chip + i, d.chips)))

    for i in range(1, d.z):
        along_z(i).wait_recv()
    fin[core, rows_of(chip)] = summed(z_v, d.z)
    for i in range(1, d.chips):
        start(spread(chip, i))

    @pl.when(has_extra)
    def _():
        for i in range(1, d.z):
            along_z_extra(i).wait_recv()
        fin[core, tile_of(spare)] = summed(z_w, d.z)
        for i in range(1, d.chips):
            spread_extra(spare, i).start()

    proj_z.wait_recv()
    px_v[x] = (pz_v[0].astype(F32) + pz_v[1].astype(F32)).astype(BF16)

    def proj_x(i):
        return send(
            px_v.at[x], px_v.at[x], "proj_x", i, i, (lax.rem(x + i, d.x) * d.zh + zh, ty, tx)
        )

    for i in range(1, d.x):
        start(proj_x(i))

    for i in range(1, d.chips):
        spread(lax.rem(chip + i, d.chips), 0).wait_recv()
    for e in range(d.extra):
        pl.when(spare != e)(spread_extra(e, 0).wait_recv)
    back_core = send(fin.at[core], fin.at[core], "core_back", 0, 0, other_core)
    start(back_core)

    for i in range(1, d.x):
        proj_x(i).wait_recv()
    total = px_v[0].astype(F32)
    for i in range(1, d.x):
        total = total + px_v[i].astype(F32)
    proj_out[:, :half] = total[:8]
    proj_out[:, half:] = total[8:]

    back_core.wait_recv()
    out_weight = local(fin, weight_out, 17)

    for when, copy in sent:
        if when is None:
            copy.wait_send()
        else:
            pl.when(when)(copy.wait_send)

    @pl.when(has_extra)
    def _():
        for i in range(1, d.z):
            along_z_extra(i).wait_send()
        for i in range(1, d.chips):
            spread_extra(spare, i).wait_send()

    for t in range(d.ty):
        for i in range(1, d.y):
            tok_y(i, t).wait_send()

    out_feature.wait()
    out_weight.wait()


def outputs(d, feature, weight, token, proj, feature_out, weight_out, token_out, proj_out, *scratch):
    weight_v, high_v, feature_v, token_v, proj_v, sem_in, sem_out = scratch
    parts = [(weight, weight_v)]
    moves = []
    step = d.rows // OUT_PARTS
    for i in range(OUT_PARTS):
        here = pl.ds(i * step, step)
        moves.append((feature.at[0, here], feature_v.at[here], feature_out.at[0, here]))
    moves.append((token, token_v, token_out))
    moves.append((proj, proj_v, proj_out))
    parts += [m[:2] for m in moves]
    ins = [pltpu.make_async_copy(a, b, sem_in.at[i]) for i, (a, b) in enumerate(parts)]
    for copy in ins:
        copy.start()
    ins[0].wait()
    high_v[...] = weight_v[...].astype(F32)
    outs = [pltpu.make_async_copy(high_v, weight_out, sem_out.at[0])]
    outs[0].start()
    for i, (_, b, c) in enumerate(moves):
        ins[i + 1].wait()
        outs.append(pltpu.make_async_copy(b, c, sem_out.at[i + 1]))
        outs[-1].start()
    for copy in outs:
        copy.wait()


def shards(d, *args):
    tile = (d.rows, d.cols, LANES)
    half = 3 * d.width // 2
    blocks = d.width // LANES
    packed = d.tok * blocks
    assert packed == TILE and d.rows == TILE
    _, messages = message_slots(d)
    hbm = pl.BlockSpec(memory_space=pl.ANY)
    vmem = pl.BlockSpec(memory_space=pltpu.VMEM)
    results = pl.pallas_call(
        functools.partial(kernel, d),
        out_shape=(
            jax.ShapeDtypeStruct((1, *tile), BF16),
            jax.ShapeDtypeStruct((CORES, d.half, LANES), BF16),
            jax.ShapeDtypeStruct((1, d.tok, d.width), BF16),
            jax.ShapeDtypeStruct((8, 3 * d.width), F32),
        ),
        in_specs=[hbm] * 8,
        out_specs=(hbm, hbm, vmem, vmem),
        scratch_shapes=[
            pltpu.VMEM(tile, BF16),
            pltpu.VMEM((d.rows + 2, d.cols, LANES), BF16),
            pltpu.VMEM((d.rows + 2, d.cols, 3 * LANES), BF16),
            pltpu.VMEM((LANES, 9 * LANES), BF16),
            pltpu.VMEM((3, d.width, d.width), BF16),
            pltpu.VMEM(tile, BF16),
            pltpu.VMEM((LANES, 9 * LANES), F32),
            pltpu.VMEM((9 * LANES, LANES), F32),
            pltpu.VMEM((d.half, LANES), BF16),
            pltpu.VMEM((d.half, LANES), BF16),
            pltpu.VMEM((d.half, LANES), BF16),
            pltpu.VMEM((d.chips, d.piece, LANES), BF16),
            pltpu.VMEM((d.z, d.piece, LANES), BF16),
            pltpu.VMEM((d.chips, TILE, LANES), BF16),
            pltpu.VMEM((d.z, TILE, LANES), BF16),
            pltpu.VMEM((CORES, d.half, LANES), BF16),
            pltpu.VMEM((2, d.rows, LANES), BF16),
            pltpu.VMEM((2, 3, d.rows, LANES), BF16),
            pltpu.VMEM((2, d.rows + 8, LANES), F32),
            pltpu.VMEM((2, d.tok, d.width), BF16),
            pltpu.VMEM((2, packed, LANES), F32),
            pltpu.VMEM((CORES, 2, d.y, d.ty, packed, LANES), BF16),
            pltpu.VMEM((d.tokens * blocks // CORES, LANES), F32),
            pltpu.VMEM((2, d.tokens, d.width), BF16),
            pltpu.VMEM((d.tokens, 3 * d.width), BF16),
            pltpu.VMEM((d.tokens, 3 * d.width), BF16),
            pltpu.VMEM((d.zh, 16, half), BF16),
            pltpu.VMEM((d.x, 16, half), BF16),
            pltpu.SemaphoreType.DMA((18,)),
            pltpu.SemaphoreType.DMA((messages,)),
            pltpu.SemaphoreType.DMA((messages,)),
        ],
        compiler_params=pltpu.CompilerParams(
            collective_id=0, has_side_effects=True, vmem_limit_bytes=VMEM_LIMIT
        ),
    )(*args)
    feature_grad, conv_weight_grad, token_grad, proj_grad = pl.pallas_call(
        functools.partial(outputs, d),
        out_shape=(
            jax.ShapeDtypeStruct((1, *tile), BF16),
            jax.ShapeDtypeStruct((CORES, d.half, LANES), F32),
            jax.ShapeDtypeStruct((1, d.tok, d.width), BF16),
            jax.ShapeDtypeStruct((8, 3 * d.width), F32),
        ),
        in_specs=[hbm] * 4,
        out_specs=(hbm,) * 4,
        scratch_shapes=[
            pltpu.VMEM((CORES, d.half, LANES), BF16),
            pltpu.VMEM((CORES, d.half, LANES), F32),
            pltpu.VMEM(tile, BF16),
            pltpu.VMEM((1, d.tok, d.width), BF16),
            pltpu.VMEM((8, 3 * d.width), F32),
            pltpu.SemaphoreType.DMA((OUT_PARTS + 3,)),
            pltpu.SemaphoreType.DMA((OUT_PARTS + 3,)),
        ],
        compiler_params=pltpu.CompilerParams(vmem_limit_bytes=VMEM_LIMIT),
    )(*results)
    return feature_grad, conv_weight_grad.reshape(3, 3, LANES, LANES), token_grad, proj_grad


def solution(mesh):
    sizes = mesh.shape
    zh = 2

    def whole(*args):
        _, height, width, _ = args[0].shape
        _, tokens, channels = args[3].shape
        d = Dims(
            x=sizes["rep"] // zh,
            zh=zh,
            ty=sizes["ty"],
            y=sizes["tx"] // CORES,
            rows=height // sizes["ty"],
            cols=width // sizes["tx"],
            tok=tokens // (sizes["ty"] * sizes["tx"]),
            width=channels,
        )
        in_specs = (
            P("rep", "ty", "tx", None),
            P("rep", "ty", "tx", None),
            P(),
            P("rep", ("ty", "tx"), None),
            P("rep", ("ty", "tx"), None),
            P(),
            P(),
            P(),
        )
        out_specs = (
            P("rep", "ty", "tx", None),
            P(),
            P("rep", ("ty", "tx"), None),
            P(("ty", "tx"), None),
        )
        return jax.shard_map(
            functools.partial(shards, d),
            mesh=mesh,
            in_specs=in_specs,
            out_specs=out_specs,
            check_vma=False,
        )(*args)

    return whole
```

```python
import dataclasses
import functools

import jax
import jax.numpy as jnp
from jax import lax
from jax.experimental import pallas as pl
from jax.experimental.pallas import tpu as pltpu
from jax.sharding import PartitionSpec as P

HEAD_DIM = 64
LANES = 128
TILE = 16
CORES = 2
EARLY = 4
VMEM_LIMIT = 60 * 1024 * 1024
MESH = pl.DeviceIdType.MESH
BF16 = jnp.bfloat16
F32 = jnp.float32

NN = (((1,), (0,)), ((), ()))
NT = (((1,), (1,)), ((), ()))
TN = (((0,), (0,)), ((), ()))


def dot(a, b, dims):
    return lax.dot_general(a, b, dims, preferred_element_type=F32)


@dataclasses.dataclass(frozen=True)
class Dims:
    x: int
    zh: int
    ty: int
    y: int
    rows: int
    cols: int
    tok: int
    width: int

    @property
    def z(self):
        return self.zh * self.ty

    @property
    def tx(self):
        return self.y * CORES

    @property
    def chips(self):
        return self.x * self.y

    @property
    def half(self):
        return 9 * LANES // CORES

    @property
    def piece(self):
        return (self.half // TILE - 1) // self.chips * TILE

    @property
    def extra(self):
        return self.half // TILE - self.chips * (self.piece // TILE)

    @property
    def tokens(self):
        return self.ty * self.tx * self.tok


def message_slots(d):
    slots = {}
    count = 0
    for name, n in (
        ("row", 2),
        ("col", 6),
        ("tok_z", d.ty),
        ("tok_y", d.y * d.ty),
        ("tok_core", 1),
        ("core", 1),
        ("plane", d.chips),
        ("along_z", d.z),
        ("spread", d.chips),
        ("plane_extra", d.chips),
        ("along_z_extra", d.z),
        ("spread_extra", d.chips),
        ("core_back", 1),
        ("proj_z", 1),
        ("proj_x", d.x),
    ):
        slots[name] = count
        count += n
    return slots, count


def kernel(
    d,
    features,
    fine_grad,
    conv_weight,
    bottom,
    bottom_grad,
    query_weight,
    key_weight,
    value_weight,
    feature_out,
    weight_out,
    token_out,
    proj_out,
    feat_v,
    grad_v,
    shifted,
    taps,
    proj_w,
    acc,
    flat,
    core_send,
    core_v,
    half_v,
    plane_v,
    z_v,
    plane_w,
    z_w,
    col_send,
    col_recv,
    col_halo,
    tok_v,
    pack_v,
    gath,
    wide,
    tok_all,
    qkv,
    pgrad,
    pz_v,
    px_v,
    local_sem,
    send_sem,
    recv_sem,
):
    slots, _ = message_slots(d)
    rows, cols = d.rows, d.cols
    rep, ty, tx = (lax.axis_index(a) for a in ("rep", "ty", "tx"))
    x, zh = rep // d.zh, rep % d.zh
    y, core = tx // CORES, tx % CORES
    z = zh * d.ty + ty
    chip = y * d.x + x

    def at_chip(c):
        return (lax.rem(c, d.x) * d.zh + zh, ty, (c // d.x) * CORES + core)

    def at_z(k):
        return (x * d.zh + k // d.ty, lax.rem(k, d.ty), tx)

    def at_tx(t):
        return (rep, ty, t)

    def at_ty(t):
        return (rep, t, tx)

    other_core = at_tx(y * CORES + 1 - core)

    def send(src, dst, name, out_index, in_index, device):
        return pltpu.make_async_remote_copy(
            src_ref=src,
            dst_ref=dst,
            send_sem=send_sem.at[slots[name] + out_index],
            recv_sem=recv_sem.at[slots[name] + in_index],
            device_id=device,
            device_id_type=MESH,
        )

    sent = []

    def start(copy, when=None):
        sent.append((when, copy))
        if when is None:
            copy.start()
        else:
            pl.when(when)(copy.start)

    def local(src, dst, i):
        copy = pltpu.make_async_copy(src, dst, local_sem.at[i])
        copy.start()
        return copy

    in_tok = [local(bottom.at[0], tok_v.at[0], 0), local(bottom_grad.at[0], tok_v.at[1], 1)]
    in_grad = local(fine_grad.at[0], grad_v.at[pl.ds(1, rows)], 2)
    in_feat = local(features.at[0], feat_v, 3)

    barrier = pltpu.get_barrier_semaphore()
    peers = [other_core]
    peers += [at_tx(lax.rem(tx + i, d.tx)) for i in (1, d.tx - 1)]
    peers += [at_chip(lax.rem(chip + i, d.chips)) for i in range(1, d.chips)]
    far = sorted(range(1, d.z), key=lambda i: min(i, d.z - i))
    for dy in (1, d.ty - 1):
        for dx in (1, d.tx - 1):
            peers.append((rep, lax.rem(ty + dy, d.ty), lax.rem(tx + dx, d.tx)))
    peers += [at_z(lax.rem(z + i, d.z)) for i in far]
    for peer in reversed(peers):
        pl.semaphore_signal(barrier, inc=1, device_id=peer, device_id_type=MESH)

    in_taps = [
        local(conv_weight.at[k // 3, k % 3], taps.at[:, pl.ds(k * LANES, LANES)], 7 + k)
        for k in range(9)
    ]
    in_proj = [
        local(w, proj_w.at[i], 4 + i) for i, w in enumerate((query_weight, key_weight, value_weight))
    ]

    blocks = d.width // LANES
    for i, copy in enumerate(in_tok):
        copy.wait()
        mine = tok_v[i].astype(F32)
        for c in range(blocks):
            pack_v[i, pl.ds(c, d.tok, stride=blocks), :] = mine[:, c * LANES : (c + 1) * LANES]
        gath[core, i, y, ty] = pack_v[i].astype(BF16)
    in_grad.wait()
    lane_rows = lax.broadcasted_iota(jnp.int32, (rows, TILE, LANES), 1)

    def column(ref, first, side):
        base, row = ((0, 0), (cols - TILE, TILE - 1))[side]
        edge = ref[first : first + rows, base : base + TILE, :].astype(F32)
        return jnp.sum(jnp.where(lane_rows == row, edge, 0.0), axis=1)

    for side in range(2):
        col_send[side] = column(grad_v, 1, side).astype(BF16)

    col_halo[...] = jnp.zeros_like(col_halo)
    col_index = lax.broadcasted_iota(jnp.int32, (cols, LANES), 0)

    def shift_row(r, carry):
        line = grad_v[r]
        wide_line = line.astype(F32)
        before = jnp.where(col_index == 0, col_halo[0, pl.ds(r, 1)], pltpu.roll(wide_line, 1, 0))
        after = jnp.where(
            col_index == cols - 1, col_halo[1, pl.ds(r, 1)], pltpu.roll(wide_line, cols - 1, 0)
        )
        shifted[r, :, 0:LANES] = after.astype(BF16)
        shifted[r, :, LANES : 2 * LANES] = line
        shifted[r, :, 2 * LANES :] = before.astype(BF16)
        return carry

    lax.fori_loop(1, rows + 1, shift_row, 0)
    for r in (0, rows + 1):
        shifted[r] = jnp.zeros((cols, 3 * LANES), BF16)
    in_feat.wait()

    group = 4
    pixels = group * cols

    def neighbours(r):
        return jnp.concatenate(
            [
                shifted[pl.ds(r + 2 - ky, group)].reshape(pixels, 3 * LANES)
                for ky in range(3)
            ],
            axis=-1,
        )

    def silu(v):
        value = v.astype(F32)
        return (value * jax.nn.sigmoid(value)).astype(BF16)

    acc[...] = jnp.zeros_like(acc)

    def weight_step(i, carry):
        active = silu(feat_v[pl.ds(i * group, group)].reshape(pixels, LANES))
        acc[...] += dot(active, neighbours(i * group), TN)
        return carry

    lax.fori_loop(0, EARLY, weight_step, 0)

    pl.semaphore_wait(barrier, len(peers))

    up, down = ty > 0, ty < d.ty - 1
    left, right = tx > 0, tx < d.tx - 1
    upper, lower = lax.rem(ty + d.ty - 1, d.ty), lax.rem(ty + 1, d.ty)
    row_up = send(grad_v.at[1], grad_v.at[rows + 1], "row", 0, 1, at_ty(upper))
    row_down = send(grad_v.at[rows], grad_v.at[0], "row", 1, 0, at_ty(lower))
    start(row_up, up)
    start(row_down, down)
    arrivals = []
    for side, there, out_ok, in_ok in (
        (0, lax.rem(tx + d.tx - 1, d.tx), left, right),
        (1, lax.rem(tx + 1, d.tx), right, left),
    ):
        for dy, there_y, out_y, in_y in (
            (0, upper, up, down),
            (1, ty, True, True),
            (2, lower, down, up),
        ):
            copy = send(
                col_send.at[side],
                col_recv.at[1 - side, 2 - dy],
                "col",
                side * 3 + dy,
                (1 - side) * 3 + 2 - dy,
                (rep, there_y, there),
            )
            start(copy, jnp.logical_and(out_ok, out_y))
            arrivals.append((jnp.logical_and(in_ok, in_y), copy, 1 - side, 2 - dy))

    def tok_z(i):
        mine = gath.at[core, :, y, ty]
        return send(mine, mine, "tok_z", i, ty, at_ty(lax.rem(ty + i, d.ty)))

    def tok_z_from(t):
        there = gath.at[core, :, y, t]
        return send(there, there, "tok_z", 0, t, at_ty(t))

    def tok_y(i, t):
        tile = gath.at[core, :, y, t]
        k = i * d.ty + t
        return send(tile, tile, "tok_y", k, k, at_tx(lax.rem(tx + i * CORES, d.tx)))

    for i in range(1, d.ty):
        start(tok_z(i))
    for i in range(1, d.y):
        tok_y(i, ty).start()

    lax.fori_loop(EARLY, rows // group, weight_step, 0)

    @pl.when(jnp.logical_not(up))
    def _():
        grad_v[0] = jnp.zeros((cols, LANES), BF16)

    @pl.when(jnp.logical_not(down))
    def _():
        grad_v[rows + 1] = jnp.zeros((cols, LANES), BF16)

    pl.when(up)(row_down.wait_recv)
    pl.when(down)(row_up.wait_recv)
    for ok, copy, side, place in arrivals:

        @pl.when(ok)
        def _(copy=copy, side=side, place=place):
            copy.wait_recv()
            tile = col_recv[side, place].astype(F32)
            if place == 0:
                col_halo[side, 0:1] = tile[rows - 1 : rows]
            elif place == 1:
                col_halo[side, 1 : rows + 1] = tile
            else:
                col_halo[side, rows + 1 : rows + 2] = tile[0:1]

    for r, inner, ky in ((0, 0, 2), (rows + 1, rows - 1, 0)):
        shift_row(r, 0)
        acc[:, ky * 3 * LANES : (ky + 1) * 3 * LANES] += dot(silu(feat_v[inner]), shifted[r], TN)
    halo_row = lax.broadcasted_iota(jnp.int32, (rows + 8, LANES), 0)
    inside = jnp.logical_and(halo_row >= 1, halo_row <= rows)
    for side, kx in ((0, 2), (1, 0)):
        active = silu(column(feat_v, 0, side))
        line = jnp.where(inside, col_halo[side], 0.0)
        three = jnp.concatenate([line[2 - ky : 2 - ky + rows] for ky in range(3)], axis=1)
        more = dot(active, three.astype(BF16), TN)
        for ky in range(3):
            k = ky * 3 + kx
            acc[:, k * LANES : (k + 1) * LANES] += more[:, ky * LANES : (ky + 1) * LANES]
    for k in range(9):
        flat[k * LANES : (k + 1) * LANES, :] = acc[:, k * LANES : (k + 1) * LANES]

    def core_rows(c):
        return pl.ds(pl.multiple_of(c * d.half, TILE), d.half)

    core_send[...] = flat[core_rows(1 - core), :].astype(BF16)
    to_core = send(core_send, core_v, "core", 0, 0, other_core)
    start(to_core)

    tile_row = lax.broadcasted_iota(jnp.int32, (TILE, LANES), 0)

    def fix_row(r, carry):
        for side, base, lanes, row in ((0, 0, 2 * LANES, 0), (1, cols - TILE, 0, TILE - 1)):
            here = (r, pl.ds(base, TILE), pl.ds(lanes, LANES))
            tile = shifted[here].astype(F32)
            tile = jnp.where(tile_row == row, col_halo[side, pl.ds(r, 1)], tile)
            shifted[here] = tile.astype(BF16)
        return carry

    lax.fori_loop(1, rows + 1, fix_row, 0)

    to_core.wait_recv()
    half_v[...] = (flat[core_rows(core), :] + core_v[...].astype(F32)).astype(BF16)

    spare = lax.rem(chip + core * (d.chips - d.extra), d.chips)
    has_extra = spare < d.extra
    last = d.chips * d.piece

    def turned(e):
        return lax.rem(e + core * d.extra, d.chips)

    def rows_of(c):
        return pl.ds(pl.multiple_of(c * d.piece, TILE), d.piece)

    def tile_of(e):
        return pl.ds(pl.multiple_of(last + e * TILE, TILE), TILE)

    def to_plane(i):
        there = lax.rem(chip + i, d.chips)
        return send(
            half_v.at[rows_of(there)], plane_v.at[chip], "plane", i, chip, at_chip(there)
        )

    def from_plane(i):
        there = lax.rem(chip + i, d.chips)
        return send(
            half_v.at[rows_of(there)], plane_v.at[there], "plane", i, there, at_chip(there)
        )

    def to_plane_extra(e):
        there = turned(e)
        return send(
            half_v.at[tile_of(e)], plane_w.at[chip], "plane_extra", e, chip, at_chip(there)
        )

    def from_plane_extra(i):
        there = lax.rem(chip + i, d.chips)
        return send(
            half_v.at[tile_of(0)], plane_w.at[there], "plane_extra", 0, there, at_chip(there)
        )

    for i in range(1, d.chips):
        start(to_plane(i))
    for e in range(d.extra):
        start(to_plane_extra(e), spare != e)

    for distance in range(1, d.ty):
        for t in (ty + distance, ty - distance):

            @pl.when(jnp.logical_and(t >= 0, t < d.ty))
            def _(t=t):
                tok_z_from(t).wait_recv()
                for i in range(1, d.y):
                    tok_y(i, t).start()

    def along_z(i):
        return send(z_v.at[z], z_v.at[z], "along_z", i, i, at_z(lax.rem(z + i, d.z)))

    def along_z_extra(i):
        return send(z_w.at[z], z_w.at[z], "along_z_extra", i, i, at_z(lax.rem(z + i, d.z)))

    def summed(ref, count):
        total = ref[0].astype(F32)
        for i in range(1, count):
            total = total + ref[i].astype(F32)
        return total.astype(BF16)

    plane_v[chip] = half_v[rows_of(chip), :]
    for i in range(1, d.chips):
        from_plane(i).wait_recv()
    z_v[z] = summed(plane_v, d.chips)
    for i in range(1, d.z):
        start(along_z(i))

    @pl.when(has_extra)
    def _():
        plane_w[chip] = half_v[tile_of(spare), :]
        for i in range(1, d.chips):
            from_plane_extra(i).wait_recv()
        z_w[z] = summed(plane_w, d.chips)
        for i in range(1, d.z):
            along_z_extra(i).start()

    for t in range(d.ty):
        for i in range(1, d.y):
            tok_y(i, t).wait_recv()
    to_core_tok = send(gath.at[core], gath.at[core], "tok_core", 0, 0, other_core)
    start(to_core_tok)

    share = d.tokens // CORES
    for copy in in_proj:
        copy.wait()
    for c in (core, 1 - core):
        here = pl.ds(pl.multiple_of(c * share, TILE), share)
        if c is not core:
            to_core_tok.wait_recv()
        for i in range(2):
            wide[...] = gath[c, i].reshape(share * blocks, LANES).astype(F32)
            for b in range(blocks):
                tok_all[i, here, b * LANES : (b + 1) * LANES] = wide[
                    pl.ds(b, share, stride=blocks), :
                ].astype(BF16)
        for i in range(3):
            qkv[here, i * d.width : (i + 1) * d.width] = dot(
                tok_all[0, here], proj_w[i], NN
            ).astype(BF16)

    lane = lax.broadcasted_iota(jnp.int32, (d.tokens, LANES), 1)
    low = lane < HEAD_DIM
    scale = 1.0 / HEAD_DIM**0.5

    def head_pair(p, carry):
        def block(ref, offset):
            return ref[:, pl.ds(pl.multiple_of(offset + p * LANES, LANES), LANES)]

        def halves(v):
            zero = jnp.zeros_like(v)
            return jnp.concatenate([jnp.where(low, v, zero), jnp.where(low, zero, v)], axis=0)

        key = block(qkv, d.width)
        value = block(qkv, 2 * d.width)
        query2 = halves(block(qkv, 0))
        upstream2 = halves(block(tok_all.at[1], 0))
        scores = dot(key, query2, NT) * scale
        expos = jnp.exp(scores - jnp.max(scores, axis=0, keepdims=True))
        probs = expos / jnp.sum(expos, axis=0, keepdims=True)
        dprobs = dot(value, upstream2, NT)
        dscores = probs * (dprobs - jnp.sum(dprobs * probs, axis=0, keepdims=True))
        dscores_low = (dscores * scale).astype(BF16)
        value_grad = dot(probs.astype(BF16), upstream2, NN)
        key_grad = dot(dscores_low, query2, NN)
        both = dot(dscores_low, key, TN)
        query_grad = jnp.where(low, both[: d.tokens], both[d.tokens :])
        for i, g in enumerate((query_grad, key_grad, value_grad)):
            here = pl.ds(pl.multiple_of(i * d.width + p * LANES, LANES), LANES)
            pgrad[:, here] = g.astype(BF16)
        return carry

    lax.fori_loop(0, d.width // LANES, head_pair, 0)

    place = ((core * d.y + y) * d.ty + ty) * d.tok
    channel = (ty * d.tx + tx) * (d.width // (d.ty * d.tx))
    pick_row = lax.broadcasted_iota(jnp.int32, (2 * 8, d.width), 0)
    pick_col = lax.broadcasted_iota(jnp.int32, (2 * 8, d.width), 1)
    pick = jnp.logical_and(pick_col == channel + pick_row, pick_row < 8).astype(F32).astype(BF16)
    columns = dot(pick, tok_all[0], NT)
    own_row = lax.broadcasted_iota(jnp.int32, (2 * 8, d.tokens), 0)
    own_col = lax.broadcasted_iota(jnp.int32, (2 * 8, d.tokens), 1)
    picked = jnp.where(
        own_row < 8, columns, (own_col == place + own_row - 8).astype(F32)
    ).astype(BF16)
    both = dot(picked, pgrad[...], NN)
    half = 3 * d.width // 2
    pz_v[zh] = jnp.concatenate([both[:8, :half], both[:8, half:]], axis=0).astype(BF16)
    proj_z = send(pz_v.at[zh], pz_v.at[zh], "proj_z", 0, 0, at_z(lax.rem(z + d.ty, d.z)))
    start(proj_z)
    own_grads = both[8:].astype(BF16)
    back = jnp.zeros((8, d.width), F32)
    for i in range(3):
        back = back + dot(own_grads[:, i * d.width : (i + 1) * d.width], proj_w[i], NT)
    token_out[0] = (tok_v[1].astype(F32) + back[: d.tok]).astype(BF16)

    for copy in in_taps:
        copy.wait()

    def feature_step(i, carry):
        here = pl.ds(i * group, group)
        value = feat_v[here].reshape(pixels, LANES).astype(F32)
        gate = jax.nn.sigmoid(value)
        slope = gate * (1.0 + value * (1.0 - gate))
        act_grad = dot(neighbours(i * group), taps[...], NT)
        upstream = grad_v[pl.ds(i * group + 1, group)].reshape(pixels, LANES).astype(F32)
        feature_out[0, here] = (upstream + slope * act_grad).astype(BF16).reshape(group, cols, LANES)
        return carry

    lax.fori_loop(0, rows // group, feature_step, 0)

    def spread(c, i):
        here = weight_out.at[core, rows_of(c)]
        return send(here, here, "spread", i, c, at_chip(lax.rem(chip + i, d.chips)))

    def spread_extra(e, i):
        here = weight_out.at[core, tile_of(e)]
        return send(here, here, "spread_extra", i, e, at_chip(lax.rem(chip + i, d.chips)))

    for i in range(1, d.z):
        along_z(i).wait_recv()
    weight_out[core, rows_of(chip)] = summed(z_v, d.z)
    for i in range(1, d.chips):
        start(spread(chip, i))

    @pl.when(has_extra)
    def _():
        for i in range(1, d.z):
            along_z_extra(i).wait_recv()
        weight_out[core, tile_of(spare)] = summed(z_w, d.z)
        for i in range(1, d.chips):
            spread_extra(spare, i).start()

    proj_z.wait_recv()
    px_v[x] = (pz_v[0].astype(F32) + pz_v[1].astype(F32)).astype(BF16)

    def proj_x(i):
        return send(
            px_v.at[x], px_v.at[x], "proj_x", i, i, (lax.rem(x + i, d.x) * d.zh + zh, ty, tx)
        )

    for i in range(1, d.x):
        start(proj_x(i))

    for i in range(1, d.chips):
        spread(lax.rem(chip + i, d.chips), 0).wait_recv()
    for e in range(d.extra):
        pl.when(spare != e)(spread_extra(e, 0).wait_recv)
    back_core = send(weight_out.at[core], weight_out.at[core], "core_back", 0, 0, other_core)
    start(back_core)

    for i in range(1, d.x):
        proj_x(i).wait_recv()
    total = px_v[0].astype(F32)
    for i in range(1, d.x):
        total = total + px_v[i].astype(F32)
    proj_out[:, :half] = total[:8]
    proj_out[:, half:] = total[8:]

    back_core.wait_recv()

    for when, copy in sent:
        if when is None:
            copy.wait_send()
        else:
            pl.when(when)(copy.wait_send)

    @pl.when(has_extra)
    def _():
        for i in range(1, d.z):
            along_z_extra(i).wait_send()
        for i in range(1, d.chips):
            spread_extra(spare, i).wait_send()

    for t in range(d.ty):
        for i in range(1, d.y):
            tok_y(i, t).wait_send()


def outputs(feature, weight, token, proj, feature_out, weight_out, token_out, proj_out, high_v, sem):
    copies = [
        pltpu.make_async_copy(src, dst, sem.at[i])
        for i, (src, dst) in enumerate(
            ((feature, feature_out), (token, token_out), (proj, proj_out), (high_v, weight_out))
        )
    ]
    for copy in copies[:-1]:
        copy.start()
    high_v[...] = weight[...].astype(F32)
    copies[-1].start()
    for copy in copies:
        copy.wait()


def shards(d, *args):
    tile = (d.rows, d.cols, LANES)
    half = 3 * d.width // 2
    blocks = d.width // LANES
    packed = d.tok * blocks
    assert packed == TILE and d.rows == TILE
    _, messages = message_slots(d)
    hbm = pl.BlockSpec(memory_space=pl.ANY)
    vmem = pl.BlockSpec(memory_space=pltpu.VMEM)
    args = [pltpu.with_memory_space_constraint(a, pltpu.HBM) for a in args]
    results = pl.pallas_call(
        functools.partial(kernel, d),
        out_shape=(
            pltpu.VMEM((1, *tile), BF16),
            pltpu.VMEM((CORES, d.half, LANES), BF16),
            pltpu.VMEM((1, d.tok, d.width), BF16),
            pltpu.VMEM((8, 3 * d.width), F32),
        ),
        in_specs=[hbm] * 8,
        out_specs=(vmem,) * 4,
        scratch_shapes=[
            pltpu.VMEM(tile, BF16),
            pltpu.VMEM((d.rows + 2, d.cols, LANES), BF16),
            pltpu.VMEM((d.rows + 2, d.cols, 3 * LANES), BF16),
            pltpu.VMEM((LANES, 9 * LANES), BF16),
            pltpu.VMEM((3, d.width, d.width), BF16),
            pltpu.VMEM((LANES, 9 * LANES), F32),
            pltpu.VMEM((9 * LANES, LANES), F32),
            pltpu.VMEM((d.half, LANES), BF16),
            pltpu.VMEM((d.half, LANES), BF16),
            pltpu.VMEM((d.half, LANES), BF16),
            pltpu.VMEM((d.chips, d.piece, LANES), BF16),
            pltpu.VMEM((d.z, d.piece, LANES), BF16),
            pltpu.VMEM((d.chips, TILE, LANES), BF16),
            pltpu.VMEM((d.z, TILE, LANES), BF16),
            pltpu.VMEM((2, d.rows, LANES), BF16),
            pltpu.VMEM((2, 3, d.rows, LANES), BF16),
            pltpu.VMEM((2, d.rows + 8, LANES), F32),
            pltpu.VMEM((2, d.tok, d.width), BF16),
            pltpu.VMEM((2, packed, LANES), F32),
            pltpu.VMEM((CORES, 2, d.y, d.ty, packed, LANES), BF16),
            pltpu.VMEM((d.tokens * blocks // CORES, LANES), F32),
            pltpu.VMEM((2, d.tokens, d.width), BF16),
            pltpu.VMEM((d.tokens, 3 * d.width), BF16),
            pltpu.VMEM((d.tokens, 3 * d.width), BF16),
            pltpu.VMEM((d.zh, 16, half), BF16),
            pltpu.VMEM((d.x, 16, half), BF16),
            pltpu.SemaphoreType.DMA((16,)),
            pltpu.SemaphoreType.DMA((messages,)),
            pltpu.SemaphoreType.DMA((messages,)),
        ],
        compiler_params=pltpu.CompilerParams(
            collective_id=0, has_side_effects=True, vmem_limit_bytes=VMEM_LIMIT
        ),
    )(*args)
    results = [pltpu.with_memory_space_constraint(r, pltpu.VMEM) for r in results]
    feature_grad, conv_weight_grad, token_grad, proj_grad = pl.pallas_call(
        outputs,
        out_shape=(
            jax.ShapeDtypeStruct((1, *tile), BF16),
            jax.ShapeDtypeStruct((CORES, d.half, LANES), F32),
            jax.ShapeDtypeStruct((1, d.tok, d.width), BF16),
            jax.ShapeDtypeStruct((8, 3 * d.width), F32),
        ),
        in_specs=[vmem] * 4,
        out_specs=(hbm,) * 4,
        scratch_shapes=[
            pltpu.VMEM((CORES, d.half, LANES), F32),
            pltpu.SemaphoreType.DMA((4,)),
        ],
        compiler_params=pltpu.CompilerParams(vmem_limit_bytes=VMEM_LIMIT),
    )(*results)
    return feature_grad, conv_weight_grad.reshape(3, 3, LANES, LANES), token_grad, proj_grad


def solution(mesh):
    sizes = mesh.shape
    zh = 2

    def whole(*args):
        _, height, width, _ = args[0].shape
        _, tokens, channels = args[3].shape
        d = Dims(
            x=sizes["rep"] // zh,
            zh=zh,
            ty=sizes["ty"],
            y=sizes["tx"] // CORES,
            rows=height // sizes["ty"],
            cols=width // sizes["tx"],
            tok=tokens // (sizes["ty"] * sizes["tx"]),
            width=channels,
        )
        in_specs = (
            P("rep", "ty", "tx", None),
            P("rep", "ty", "tx", None),
            P(),
            P("rep", ("ty", "tx"), None),
            P("rep", ("ty", "tx"), None),
            P(),
            P(),
            P(),
        )
        out_specs = (
            P("rep", "ty", "tx", None),
            P(),
            P("rep", ("ty", "tx"), None),
            P(("ty", "tx"), None),
        )
        return jax.shard_map(
            functools.partial(shards, d),
            mesh=mesh,
            in_specs=in_specs,
            out_specs=out_specs,
            check_vma=False,
        )(*args)

    return whole
```

```python
import dataclasses
import functools

import jax
import jax.numpy as jnp
from jax import lax
from jax.experimental import pallas as pl
from jax.experimental.pallas import tpu as pltpu
from jax.sharding import PartitionSpec as P

HEAD_DIM = 64
LANES = 128
TILE = 16
CORES = 2
EARLY = 4
VMEM_LIMIT = 60 * 1024 * 1024
MESH = pl.DeviceIdType.MESH
BF16 = jnp.bfloat16
F32 = jnp.float32

NN = (((1,), (0,)), ((), ()))
NT = (((1,), (1,)), ((), ()))
TN = (((0,), (0,)), ((), ()))


def dot(a, b, dims):
    return lax.dot_general(a, b, dims, preferred_element_type=F32)


@dataclasses.dataclass(frozen=True)
class Dims:
    x: int
    zh: int
    ty: int
    y: int
    rows: int
    cols: int
    tok: int
    width: int

    @property
    def z(self):
        return self.zh * self.ty

    @property
    def tx(self):
        return self.y * CORES

    @property
    def chips(self):
        return self.x * self.y

    @property
    def half(self):
        return 9 * LANES // CORES

    @property
    def piece(self):
        return (self.half // TILE - 1) // self.chips * TILE

    @property
    def extra(self):
        return self.half // TILE - self.chips * (self.piece // TILE)

    @property
    def tokens(self):
        return self.ty * self.tx * self.tok


def message_slots(d):
    slots = {}
    count = 0
    for name, n in (
        ("row", 2),
        ("col", 6),
        ("tok_z", d.ty),
        ("tok_y", d.y * d.ty),
        ("tok_core", 1),
        ("core", 1),
        ("plane", d.chips),
        ("along_z", d.z),
        ("spread", d.chips),
        ("plane_extra", d.chips),
        ("along_z_extra", d.z),
        ("spread_extra", d.chips),
        ("core_back", 1),
        ("heads", 1),
        ("proj_z", 1),
        ("proj_x", d.x),
    ):
        slots[name] = count
        count += n
    return slots, count


def kernel(
    d,
    features,
    fine_grad,
    conv_weight,
    bottom,
    bottom_grad,
    query_weight,
    key_weight,
    value_weight,
    feature_out,
    weight_out,
    token_out,
    proj_out,
    feat_v,
    grad_v,
    shifted,
    taps,
    proj_w,
    acc,
    flat,
    core_send,
    core_v,
    half_v,
    plane_v,
    z_v,
    plane_w,
    z_w,
    col_send,
    col_recv,
    col_halo,
    tok_v,
    pack_v,
    gath,
    wide,
    tok_all,
    qkv,
    pgrad,
    head_send,
    head_v,
    pz_v,
    px_v,
    local_sem,
    send_sem,
    recv_sem,
):
    slots, _ = message_slots(d)
    rows, cols = d.rows, d.cols
    rep, ty, tx = (lax.axis_index(a) for a in ("rep", "ty", "tx"))
    x, zh = rep // d.zh, rep % d.zh
    y, core = tx // CORES, tx % CORES
    z = zh * d.ty + ty
    chip = y * d.x + x

    def at_chip(c):
        return (lax.rem(c, d.x) * d.zh + zh, ty, (c // d.x) * CORES + core)

    def at_z(k):
        return (x * d.zh + k // d.ty, lax.rem(k, d.ty), tx)

    def at_tx(t):
        return (rep, ty, t)

    def at_ty(t):
        return (rep, t, tx)

    other_core = at_tx(y * CORES + 1 - core)

    def send(src, dst, name, out_index, in_index, device):
        return pltpu.make_async_remote_copy(
            src_ref=src,
            dst_ref=dst,
            send_sem=send_sem.at[slots[name] + out_index],
            recv_sem=recv_sem.at[slots[name] + in_index],
            device_id=device,
            device_id_type=MESH,
        )

    sent = []

    def start(copy, when=None):
        sent.append((when, copy))
        if when is None:
            copy.start()
        else:
            pl.when(when)(copy.start)

    def local(src, dst, i):
        copy = pltpu.make_async_copy(src, dst, local_sem.at[i])
        copy.start()
        return copy

    in_tok = [local(bottom.at[0], tok_v.at[0], 0), local(bottom_grad.at[0], tok_v.at[1], 1)]
    in_grad = local(fine_grad.at[0], grad_v.at[pl.ds(1, rows)], 2)
    in_feat = local(features.at[0], feat_v, 3)

    barrier = pltpu.get_barrier_semaphore()
    peers = [other_core]
    peers += [at_tx(lax.rem(tx + i, d.tx)) for i in (1, d.tx - 1)]
    peers += [at_chip(lax.rem(chip + i, d.chips)) for i in range(1, d.chips)]
    far = sorted(range(1, d.z), key=lambda i: min(i, d.z - i))
    for dy in (1, d.ty - 1):
        for dx in (1, d.tx - 1):
            peers.append((rep, lax.rem(ty + dy, d.ty), lax.rem(tx + dx, d.tx)))
    peers += [at_z(lax.rem(z + i, d.z)) for i in far]
    for peer in reversed(peers):
        pl.semaphore_signal(barrier, inc=1, device_id=peer, device_id_type=MESH)

    in_taps = [
        local(conv_weight.at[k // 3, k % 3], taps.at[:, pl.ds(k * LANES, LANES)], 7 + k)
        for k in range(9)
    ]
    in_proj = [
        local(w, proj_w.at[i], 4 + i) for i, w in enumerate((query_weight, key_weight, value_weight))
    ]

    blocks = d.width // LANES
    for i, copy in enumerate(in_tok):
        copy.wait()
        mine = tok_v[i].astype(F32)
        for c in range(blocks):
            pack_v[i, pl.ds(c, d.tok, stride=blocks), :] = mine[:, c * LANES : (c + 1) * LANES]
        gath[core, i, y, ty] = pack_v[i].astype(BF16)
    in_grad.wait()
    lane_rows = lax.broadcasted_iota(jnp.int32, (rows, TILE, LANES), 1)

    def column(ref, first, side):
        base, row = ((0, 0), (cols - TILE, TILE - 1))[side]
        edge = ref[first : first + rows, base : base + TILE, :].astype(F32)
        return jnp.sum(jnp.where(lane_rows == row, edge, 0.0), axis=1)

    for side in range(2):
        col_send[side] = column(grad_v, 1, side).astype(BF16)

    col_halo[...] = jnp.zeros_like(col_halo)
    col_index = lax.broadcasted_iota(jnp.int32, (cols, LANES), 0)

    def shift_row(r, carry):
        line = grad_v[r]
        wide_line = line.astype(F32)
        before = jnp.where(col_index == 0, col_halo[0, pl.ds(r, 1)], pltpu.roll(wide_line, 1, 0))
        after = jnp.where(
            col_index == cols - 1, col_halo[1, pl.ds(r, 1)], pltpu.roll(wide_line, cols - 1, 0)
        )
        shifted[r, :, 0:LANES] = after.astype(BF16)
        shifted[r, :, LANES : 2 * LANES] = line
        shifted[r, :, 2 * LANES :] = before.astype(BF16)
        return carry

    lax.fori_loop(1, rows + 1, shift_row, 0)
    for r in (0, rows + 1):
        shifted[r] = jnp.zeros((cols, 3 * LANES), BF16)
    in_feat.wait()

    group = 4
    pixels = group * cols

    def neighbours(r):
        return jnp.concatenate(
            [
                shifted[pl.ds(r + 2 - ky, group)].reshape(pixels, 3 * LANES)
                for ky in range(3)
            ],
            axis=-1,
        )

    def silu(v):
        value = v.astype(F32)
        return (value * jax.nn.sigmoid(value)).astype(BF16)

    acc[...] = jnp.zeros_like(acc)

    def weight_step(i, carry):
        active = silu(feat_v[pl.ds(i * group, group)].reshape(pixels, LANES))
        acc[...] += dot(active, neighbours(i * group), TN)
        return carry

    lax.fori_loop(0, EARLY, weight_step, 0)

    pl.semaphore_wait(barrier, len(peers))

    up, down = ty > 0, ty < d.ty - 1
    left, right = tx > 0, tx < d.tx - 1
    upper, lower = lax.rem(ty + d.ty - 1, d.ty), lax.rem(ty + 1, d.ty)
    row_up = send(grad_v.at[1], grad_v.at[rows + 1], "row", 0, 1, at_ty(upper))
    row_down = send(grad_v.at[rows], grad_v.at[0], "row", 1, 0, at_ty(lower))
    start(row_up, up)
    start(row_down, down)
    arrivals = []
    for side, there, out_ok, in_ok in (
        (0, lax.rem(tx + d.tx - 1, d.tx), left, right),
        (1, lax.rem(tx + 1, d.tx), right, left),
    ):
        for dy, there_y, out_y, in_y in (
            (0, upper, up, down),
            (1, ty, True, True),
            (2, lower, down, up),
        ):
            copy = send(
                col_send.at[side],
                col_recv.at[1 - side, 2 - dy],
                "col",
                side * 3 + dy,
                (1 - side) * 3 + 2 - dy,
                (rep, there_y, there),
            )
            start(copy, jnp.logical_and(out_ok, out_y))
            arrivals.append((jnp.logical_and(in_ok, in_y), copy, 1 - side, 2 - dy))

    def tok_z(i):
        mine = gath.at[core, :, y, ty]
        return send(mine, mine, "tok_z", i, ty, at_ty(lax.rem(ty + i, d.ty)))

    def tok_z_from(t):
        there = gath.at[core, :, y, t]
        return send(there, there, "tok_z", 0, t, at_ty(t))

    def tok_y(i, t):
        tile = gath.at[core, :, y, t]
        k = i * d.ty + t
        return send(tile, tile, "tok_y", k, k, at_tx(lax.rem(tx + i * CORES, d.tx)))

    for i in sorted(range(1, d.ty), key=lambda i: abs(2 * i - d.ty)):
        start(tok_z(i))
    for i in range(1, d.y):
        tok_y(i, ty).start()

    lax.fori_loop(EARLY, rows // group, weight_step, 0)

    @pl.when(jnp.logical_not(up))
    def _():
        grad_v[0] = jnp.zeros((cols, LANES), BF16)

    @pl.when(jnp.logical_not(down))
    def _():
        grad_v[rows + 1] = jnp.zeros((cols, LANES), BF16)

    pl.when(up)(row_down.wait_recv)
    pl.when(down)(row_up.wait_recv)
    for ok, copy, side, place in arrivals:

        @pl.when(ok)
        def _(copy=copy, side=side, place=place):
            copy.wait_recv()
            tile = col_recv[side, place].astype(F32)
            if place == 0:
                col_halo[side, 0:1] = tile[rows - 1 : rows]
            elif place == 1:
                col_halo[side, 1 : rows + 1] = tile
            else:
                col_halo[side, rows + 1 : rows + 2] = tile[0:1]

    for r, inner, ky in ((0, 0, 2), (rows + 1, rows - 1, 0)):
        shift_row(r, 0)
        acc[:, ky * 3 * LANES : (ky + 1) * 3 * LANES] += dot(silu(feat_v[inner]), shifted[r], TN)
    halo_row = lax.broadcasted_iota(jnp.int32, (rows + 8, LANES), 0)
    inside = jnp.logical_and(halo_row >= 1, halo_row <= rows)
    for side, kx in ((0, 2), (1, 0)):
        active = silu(column(feat_v, 0, side))
        line = jnp.where(inside, col_halo[side], 0.0)
        three = jnp.concatenate([line[2 - ky : 2 - ky + rows] for ky in range(3)], axis=1)
        more = dot(active, three.astype(BF16), TN)
        for ky in range(3):
            k = ky * 3 + kx
            acc[:, k * LANES : (k + 1) * LANES] += more[:, ky * LANES : (ky + 1) * LANES]
    for k in range(9):
        flat[k * LANES : (k + 1) * LANES, :] = acc[:, k * LANES : (k + 1) * LANES]

    def core_rows(c):
        return pl.ds(pl.multiple_of(c * d.half, TILE), d.half)

    core_send[...] = flat[core_rows(1 - core), :].astype(BF16)
    to_core = send(core_send, core_v, "core", 0, 0, other_core)
    start(to_core)

    tile_row = lax.broadcasted_iota(jnp.int32, (TILE, LANES), 0)

    def fix_row(r, carry):
        for side, base, lanes, row in ((0, 0, 2 * LANES, 0), (1, cols - TILE, 0, TILE - 1)):
            here = (r, pl.ds(base, TILE), pl.ds(lanes, LANES))
            tile = shifted[here].astype(F32)
            tile = jnp.where(tile_row == row, col_halo[side, pl.ds(r, 1)], tile)
            shifted[here] = tile.astype(BF16)
        return carry

    lax.fori_loop(1, rows + 1, fix_row, 0)

    to_core.wait_recv()
    half_v[...] = (flat[core_rows(core), :] + core_v[...].astype(F32)).astype(BF16)

    spare = lax.rem(chip + core * (d.chips - d.extra), d.chips)
    has_extra = spare < d.extra
    last = d.chips * d.piece

    def turned(e):
        return lax.rem(e + core * d.extra, d.chips)

    def rows_of(c):
        return pl.ds(pl.multiple_of(c * d.piece, TILE), d.piece)

    def tile_of(e):
        return pl.ds(pl.multiple_of(last + e * TILE, TILE), TILE)

    def to_plane(i):
        there = lax.rem(chip + i, d.chips)
        return send(
            half_v.at[rows_of(there)], plane_v.at[chip], "plane", i, chip, at_chip(there)
        )

    def from_plane(i):
        there = lax.rem(chip + i, d.chips)
        return send(
            half_v.at[rows_of(there)], plane_v.at[there], "plane", i, there, at_chip(there)
        )

    def to_plane_extra(e):
        there = turned(e)
        return send(
            half_v.at[tile_of(e)], plane_w.at[chip], "plane_extra", e, chip, at_chip(there)
        )

    def from_plane_extra(i):
        there = lax.rem(chip + i, d.chips)
        return send(
            half_v.at[tile_of(0)], plane_w.at[there], "plane_extra", 0, there, at_chip(there)
        )

    for i in range(1, d.chips):
        start(to_plane(i))
    for e in range(d.extra):
        start(to_plane_extra(e), spare != e)

    for distance in range(1, d.ty):
        for t in (ty + distance, ty - distance):

            @pl.when(jnp.logical_and(t >= 0, t < d.ty))
            def _(t=t):
                tok_z_from(t).wait_recv()
                for i in range(1, d.y):
                    tok_y(i, t).start()

    def along_z(i):
        return send(z_v.at[z], z_v.at[z], "along_z", i, i, at_z(lax.rem(z + i, d.z)))

    def along_z_extra(i):
        return send(z_w.at[z], z_w.at[z], "along_z_extra", i, i, at_z(lax.rem(z + i, d.z)))

    def summed(ref, count):
        total = ref[0].astype(F32)
        for i in range(1, count):
            total = total + ref[i].astype(F32)
        return total.astype(BF16)

    plane_v[chip] = half_v[rows_of(chip), :]
    for i in range(1, d.chips):
        from_plane(i).wait_recv()
    z_v[z] = summed(plane_v, d.chips)
    for i in reversed(far):
        start(along_z(i))

    @pl.when(has_extra)
    def _():
        plane_w[chip] = half_v[tile_of(spare), :]
        for i in range(1, d.chips):
            from_plane_extra(i).wait_recv()
        z_w[z] = summed(plane_w, d.chips)
        for i in reversed(far):
            along_z_extra(i).start()

    for t in range(d.ty):
        for i in range(1, d.y):
            tok_y(i, t).wait_recv()
    to_core_tok = send(gath.at[core], gath.at[core], "tok_core", 0, 0, other_core)
    start(to_core_tok)

    share = d.tokens // CORES
    heads = d.width // CORES
    my_heads = pl.ds(pl.multiple_of(core * heads, LANES), heads)
    for copy in in_proj:
        copy.wait()
    for c in (core, 1 - core):
        here = pl.ds(pl.multiple_of(c * share, TILE), share)
        if c is not core:
            to_core_tok.wait_recv()
        for i in range(2):
            wide[...] = gath[c, i].reshape(share * blocks, LANES).astype(F32)
            for b in range(blocks):
                tok_all[i, here, b * LANES : (b + 1) * LANES] = wide[
                    pl.ds(b, share, stride=blocks), :
                ].astype(BF16)
        for i in range(3):
            qkv[here, i * heads : (i + 1) * heads] = dot(
                tok_all[0, here], proj_w[i, :, my_heads], NN
            ).astype(BF16)

    lane = lax.broadcasted_iota(jnp.int32, (d.tokens, LANES), 1)
    low = lane < HEAD_DIM
    scale = 1.0 / HEAD_DIM**0.5

    def head_pair(p, carry):
        def block(ref, offset):
            return ref[:, pl.ds(pl.multiple_of(offset + p * LANES, LANES), LANES)]

        def halves(v):
            zero = jnp.zeros_like(v)
            return jnp.concatenate([jnp.where(low, v, zero), jnp.where(low, zero, v)], axis=0)

        key = block(qkv, heads)
        value = block(qkv, 2 * heads)
        query2 = halves(block(qkv, 0))
        upstream2 = halves(block(tok_all.at[1], core * heads))
        scores = dot(key, query2, NT) * scale
        expos = jnp.exp(scores - jnp.max(scores, axis=0, keepdims=True))
        probs = expos / jnp.sum(expos, axis=0, keepdims=True)
        dprobs = dot(value, upstream2, NT)
        dscores = probs * (dprobs - jnp.sum(dprobs * probs, axis=0, keepdims=True))
        dscores_low = (dscores * scale).astype(BF16)
        value_grad = dot(probs.astype(BF16), upstream2, NN)
        key_grad = dot(dscores_low, query2, NN)
        both = dot(dscores_low, key, TN)
        query_grad = jnp.where(low, both[: d.tokens], both[d.tokens :])
        for i, g in enumerate((query_grad, key_grad, value_grad)):
            here = pl.ds(pl.multiple_of(i * heads + p * LANES, LANES), LANES)
            pgrad[:, here] = g.astype(BF16)
        return carry

    lax.fori_loop(0, heads // LANES, head_pair, 0)

    pick_row = lax.broadcasted_iota(jnp.int32, (2 * 8, d.width), 0)
    pick_col = lax.broadcasted_iota(jnp.int32, (2 * 8, d.width), 1)
    own_row = lax.broadcasted_iota(jnp.int32, (2 * 8, d.tokens), 0)
    own_col = lax.broadcasted_iota(jnp.int32, (2 * 8, d.tokens), 1)

    def rows_for(c):
        place = ((c * d.y + y) * d.ty + ty) * d.tok
        channel = (ty * d.tx + y * CORES + c) * (d.width // (d.ty * d.tx))
        pick = jnp.logical_and(pick_col == channel + pick_row, pick_row < 8).astype(F32)
        columns = dot(pick.astype(BF16), tok_all[0], NT)
        picked = jnp.where(own_row < 8, columns, (own_col == place + own_row - 8).astype(F32))
        return dot(picked.astype(BF16), pgrad[...], NN).astype(BF16)

    head_send[...] = rows_for(1 - core)
    to_core_heads = send(head_send, head_v.at[core], "heads", 0, 0, other_core)
    start(to_core_heads)
    head_v[core] = rows_for(core)
    to_core_heads.wait_recv()
    parts = [head_v[c].astype(F32) for c in range(CORES)]
    px_v[x] = jnp.concatenate([p[:8] for p in parts], axis=0).astype(BF16)

    def proj_x(i):
        there = (lax.rem(x + i, d.x) * d.zh + zh, ty, tx)
        return send(px_v.at[x], px_v.at[x], "proj_x", i, i, there)

    for i in range(1, d.x):
        start(proj_x(i))
    back = jnp.zeros((8, d.width), F32)
    for c in range(CORES):
        own_grads = parts[c][8:].astype(BF16)
        for i in range(3):
            back = back + dot(
                own_grads[:, i * heads : (i + 1) * heads],
                proj_w[i, :, c * heads : (c + 1) * heads],
                NT,
            )
    token_out[0] = (tok_v[1].astype(F32) + back[: d.tok]).astype(BF16)

    for copy in in_taps:
        copy.wait()

    def feature_step(i, carry):
        here = pl.ds(i * group, group)
        value = feat_v[here].reshape(pixels, LANES).astype(F32)
        gate = jax.nn.sigmoid(value)
        slope = gate * (1.0 + value * (1.0 - gate))
        act_grad = dot(neighbours(i * group), taps[...], NT)
        upstream = grad_v[pl.ds(i * group + 1, group)].reshape(pixels, LANES).astype(F32)
        feature_out[0, here] = (upstream + slope * act_grad).astype(BF16).reshape(group, cols, LANES)
        return carry

    lax.fori_loop(0, rows // group, feature_step, 0)

    for i in range(1, d.x):
        proj_x(i).wait_recv()
    pz_v[zh] = summed(px_v, d.x)
    proj_z = send(pz_v.at[zh], pz_v.at[zh], "proj_z", 0, 0, at_z(lax.rem(z + d.ty, d.z)))
    start(proj_z)

    def spread(c, i):
        here = weight_out.at[core, rows_of(c)]
        return send(here, here, "spread", i, c, at_chip(lax.rem(chip + i, d.chips)))

    def spread_extra(e, i):
        here = weight_out.at[core, tile_of(e)]
        return send(here, here, "spread_extra", i, e, at_chip(lax.rem(chip + i, d.chips)))

    for i in range(1, d.z):
        along_z(i).wait_recv()
    weight_out[core, rows_of(chip)] = summed(z_v, d.z)
    for i in range(1, d.chips):
        start(spread(chip, i))

    @pl.when(has_extra)
    def _():
        for i in range(1, d.z):
            along_z_extra(i).wait_recv()
        weight_out[core, tile_of(spare)] = summed(z_w, d.z)
        for i in range(1, d.chips):
            spread_extra(spare, i).start()

    for i in range(1, d.chips):
        spread(lax.rem(chip + i, d.chips), 0).wait_recv()
    for e in range(d.extra):
        pl.when(spare != e)(spread_extra(e, 0).wait_recv)
    back_core = send(weight_out.at[core], weight_out.at[core], "core_back", 0, 0, other_core)
    start(back_core)

    proj_z.wait_recv()
    total = pz_v[0].astype(F32)
    for k in range(1, d.zh):
        total = total + pz_v[k].astype(F32)
    for i in range(3):
        for c in range(CORES):
            first = i * d.width + c * heads
            proj_out[:, first : first + heads] = total[c * 8 : c * 8 + 8, i * heads : (i + 1) * heads]

    back_core.wait_recv()

    for when, copy in sent:
        if when is None:
            copy.wait_send()
        else:
            pl.when(when)(copy.wait_send)

    @pl.when(has_extra)
    def _():
        for i in range(1, d.z):
            along_z_extra(i).wait_send()
        for i in range(1, d.chips):
            spread_extra(spare, i).wait_send()

    for t in range(d.ty):
        for i in range(1, d.y):
            tok_y(i, t).wait_send()


def outputs(feature, weight, token, proj, feature_out, weight_out, token_out, proj_out, high_v, sem):
    copies = [
        pltpu.make_async_copy(src, dst, sem.at[i])
        for i, (src, dst) in enumerate(
            ((feature, feature_out), (token, token_out), (proj, proj_out), (high_v, weight_out))
        )
    ]
    for copy in copies[:-1]:
        copy.start()
    high_v[...] = weight[...].astype(F32)
    copies[-1].start()
    for copy in copies:
        copy.wait()


def shards(d, *args):
    tile = (d.rows, d.cols, LANES)
    half = 3 * d.width // 2
    blocks = d.width // LANES
    packed = d.tok * blocks
    assert packed == TILE and d.rows == TILE
    _, messages = message_slots(d)
    hbm = pl.BlockSpec(memory_space=pl.ANY)
    vmem = pl.BlockSpec(memory_space=pltpu.VMEM)
    args = [pltpu.with_memory_space_constraint(a, pltpu.HBM) for a in args]
    results = pl.pallas_call(
        functools.partial(kernel, d),
        out_shape=(
            pltpu.VMEM((1, *tile), BF16),
            pltpu.VMEM((CORES, d.half, LANES), BF16),
            pltpu.VMEM((1, d.tok, d.width), BF16),
            pltpu.VMEM((8, 3 * d.width), F32),
        ),
        in_specs=[hbm] * 8,
        out_specs=(vmem,) * 4,
        scratch_shapes=[
            pltpu.VMEM(tile, BF16),
            pltpu.VMEM((d.rows + 2, d.cols, LANES), BF16),
            pltpu.VMEM((d.rows + 2, d.cols, 3 * LANES), BF16),
            pltpu.VMEM((LANES, 9 * LANES), BF16),
            pltpu.VMEM((3, d.width, d.width), BF16),
            pltpu.VMEM((LANES, 9 * LANES), F32),
            pltpu.VMEM((9 * LANES, LANES), F32),
            pltpu.VMEM((d.half, LANES), BF16),
            pltpu.VMEM((d.half, LANES), BF16),
            pltpu.VMEM((d.half, LANES), BF16),
            pltpu.VMEM((d.chips, d.piece, LANES), BF16),
            pltpu.VMEM((d.z, d.piece, LANES), BF16),
            pltpu.VMEM((d.chips, TILE, LANES), BF16),
            pltpu.VMEM((d.z, TILE, LANES), BF16),
            pltpu.VMEM((2, d.rows, LANES), BF16),
            pltpu.VMEM((2, 3, d.rows, LANES), BF16),
            pltpu.VMEM((2, d.rows + 8, LANES), F32),
            pltpu.VMEM((2, d.tok, d.width), BF16),
            pltpu.VMEM((2, packed, LANES), F32),
            pltpu.VMEM((CORES, 2, d.y, d.ty, packed, LANES), BF16),
            pltpu.VMEM((d.tokens * blocks // CORES, LANES), F32),
            pltpu.VMEM((2, d.tokens, d.width), BF16),
            pltpu.VMEM((d.tokens, half), BF16),
            pltpu.VMEM((d.tokens, half), BF16),
            pltpu.VMEM((2 * 8, half), BF16),
            pltpu.VMEM((CORES, 2 * 8, half), BF16),
            pltpu.VMEM((d.zh, 16, half), BF16),
            pltpu.VMEM((d.x, 16, half), BF16),
            pltpu.SemaphoreType.DMA((16,)),
            pltpu.SemaphoreType.DMA((messages,)),
            pltpu.SemaphoreType.DMA((messages,)),
        ],
        compiler_params=pltpu.CompilerParams(
            collective_id=0, has_side_effects=True, vmem_limit_bytes=VMEM_LIMIT
        ),
    )(*args)
    results = [pltpu.with_memory_space_constraint(r, pltpu.VMEM) for r in results]
    feature_grad, conv_weight_grad, token_grad, proj_grad = pl.pallas_call(
        outputs,
        out_shape=(
            jax.ShapeDtypeStruct((1, *tile), BF16),
            jax.ShapeDtypeStruct((CORES, d.half, LANES), F32),
            jax.ShapeDtypeStruct((1, d.tok, d.width), BF16),
            jax.ShapeDtypeStruct((8, 3 * d.width), F32),
        ),
        in_specs=[vmem] * 4,
        out_specs=(hbm,) * 4,
        scratch_shapes=[
            pltpu.VMEM((CORES, d.half, LANES), F32),
            pltpu.SemaphoreType.DMA((4,)),
        ],
        compiler_params=pltpu.CompilerParams(vmem_limit_bytes=VMEM_LIMIT),
    )(*results)
    return feature_grad, conv_weight_grad.reshape(3, 3, LANES, LANES), token_grad, proj_grad


def solution(mesh):
    sizes = mesh.shape
    zh = 2

    def whole(*args):
        _, height, width, _ = args[0].shape
        _, tokens, channels = args[3].shape
        d = Dims(
            x=sizes["rep"] // zh,
            zh=zh,
            ty=sizes["ty"],
            y=sizes["tx"] // CORES,
            rows=height // sizes["ty"],
            cols=width // sizes["tx"],
            tok=tokens // (sizes["ty"] * sizes["tx"]),
            width=channels,
        )
        in_specs = (
            P("rep", "ty", "tx", None),
            P("rep", "ty", "tx", None),
            P(),
            P("rep", ("ty", "tx"), None),
            P("rep", ("ty", "tx"), None),
            P(),
            P(),
            P(),
        )
        out_specs = (
            P("rep", "ty", "tx", None),
            P(),
            P("rep", ("ty", "tx"), None),
            P(("ty", "tx"), None),
        )
        return jax.shard_map(
            functools.partial(shards, d),
            mesh=mesh,
            in_specs=in_specs,
            out_specs=out_specs,
            check_vma=False,
        )(*args)

    return whole
```

```python
import dataclasses
import functools

import jax
import jax.numpy as jnp
from jax import lax
from jax.experimental import pallas as pl
from jax.experimental.pallas import tpu as pltpu
from jax.sharding import PartitionSpec as P

HEAD_DIM = 64
LANES = 128
TILE = 16
CORES = 2
VMEM_LIMIT = 60 * 1024 * 1024
MESH = pl.DeviceIdType.MESH
BF16 = jnp.bfloat16
F32 = jnp.float32

NN = (((1,), (0,)), ((), ()))
NT = (((1,), (1,)), ((), ()))
TN = (((0,), (0,)), ((), ()))


def dot(a, b, dims):
    return lax.dot_general(a, b, dims, preferred_element_type=F32)


@dataclasses.dataclass(frozen=True)
class Dims:
    x: int
    zh: int
    ty: int
    y: int
    rows: int
    cols: int
    tok: int
    width: int

    @property
    def z(self):
        return self.zh * self.ty

    @property
    def tx(self):
        return self.y * CORES

    @property
    def chips(self):
        return self.x * self.y

    @property
    def half(self):
        return 9 * LANES // CORES

    @property
    def piece(self):
        return (self.half // TILE - 1) // self.chips * TILE

    @property
    def extra(self):
        return self.half // TILE - self.chips * (self.piece // TILE)

    @property
    def tokens(self):
        return self.ty * self.tx * self.tok


def message_slots(d):
    slots = {}
    count = 0
    for name, n in (
        ("row", 2),
        ("col", 6),
        ("tok_z", d.ty),
        ("tok_y", d.y * d.ty),
        ("tok_core", 1),
        ("core", 1),
        ("plane", d.chips),
        ("along_z", d.z),
        ("spread", d.chips),
        ("plane_extra", d.chips),
        ("along_z_extra", d.z),
        ("spread_extra", d.chips),
        ("core_back", 1),
        ("heads", 1),
        ("proj_z", 1),
        ("proj_x", d.x),
    ):
        slots[name] = count
        count += n
    return slots, count


def kernel(
    d,
    features,
    fine_grad,
    conv_weight,
    bottom,
    bottom_grad,
    query_weight,
    key_weight,
    value_weight,
    feature_out,
    weight_out,
    token_out,
    proj_out,
    feat_v,
    grad_v,
    shifted,
    taps,
    proj_w,
    acc,
    flat,
    edge_row,
    edge_col,
    core_send,
    core_v,
    half_v,
    plane_v,
    z_v,
    plane_w,
    z_w,
    col_send,
    col_recv,
    col_halo,
    tok_v,
    pack_v,
    gath,
    wide,
    tok_all,
    qkv,
    pgrad,
    head_send,
    head_v,
    pz_v,
    px_v,
    local_sem,
    send_sem,
    recv_sem,
):
    slots, _ = message_slots(d)
    rows, cols = d.rows, d.cols
    rep, ty, tx = (lax.axis_index(a) for a in ("rep", "ty", "tx"))
    x, zh = rep // d.zh, rep % d.zh
    y, core = tx // CORES, tx % CORES
    z = zh * d.ty + ty
    chip = y * d.x + x

    def at_chip(c):
        return (lax.rem(c, d.x) * d.zh + zh, ty, (c // d.x) * CORES + core)

    def at_z(k):
        return (x * d.zh + k // d.ty, lax.rem(k, d.ty), tx)

    def at_tx(t):
        return (rep, ty, t)

    def at_ty(t):
        return (rep, t, tx)

    other_core = at_tx(y * CORES + 1 - core)

    def away(o):
        return min(o[0], d.y - o[0]) + min(o[1], d.x - o[1])

    offsets = [(dy, dx) for dy in range(d.y) for dx in range(d.x) if (dy, dx) != (0, 0)]
    offsets.sort(key=away, reverse=True)

    def beside(i):
        dy, dx = offsets[i - 1]
        return lax.rem(y + dy, d.y) * d.x + lax.rem(x + dx, d.x)

    def send(src, dst, name, out_index, in_index, device):
        return pltpu.make_async_remote_copy(
            src_ref=src,
            dst_ref=dst,
            send_sem=send_sem.at[slots[name] + out_index],
            recv_sem=recv_sem.at[slots[name] + in_index],
            device_id=device,
            device_id_type=MESH,
        )

    sent = []

    def start(copy, when=None):
        sent.append((when, copy))
        if when is None:
            copy.start()
        else:
            pl.when(when)(copy.start)

    def local(src, dst, i):
        copy = pltpu.make_async_copy(src, dst, local_sem.at[i])
        copy.start()
        return copy

    in_tok = [local(bottom.at[0], tok_v.at[0], 0), local(bottom_grad.at[0], tok_v.at[1], 1)]
    in_grad = local(fine_grad.at[0], grad_v.at[pl.ds(1, rows)], 2)
    in_feat = local(features.at[0], feat_v, 3)

    barrier = pltpu.get_barrier_semaphore()
    peers = [other_core]
    peers += [at_tx(lax.rem(tx + i, d.tx)) for i in (1, d.tx - 1)]
    peers += [at_chip(beside(i)) for i in range(1, d.chips)]
    far = sorted(range(1, d.z), key=lambda i: min(i, d.z - i))
    for dy in (1, d.ty - 1):
        for dx in (1, d.tx - 1):
            peers.append((rep, lax.rem(ty + dy, d.ty), lax.rem(tx + dx, d.tx)))
    peers += [at_z(lax.rem(z + i, d.z)) for i in far]
    for peer in reversed(peers):
        pl.semaphore_signal(barrier, inc=1, device_id=peer, device_id_type=MESH)

    in_taps = [
        local(conv_weight.at[k // 3, k % 3], taps.at[:, pl.ds(k * LANES, LANES)], 7 + k)
        for k in range(9)
    ]
    in_proj = [
        local(w, proj_w.at[i], 4 + i) for i, w in enumerate((query_weight, key_weight, value_weight))
    ]

    blocks = d.width // LANES
    for i, copy in enumerate(in_tok):
        copy.wait()
        mine = tok_v[i].astype(F32)
        for c in range(blocks):
            pack_v[i, pl.ds(c, d.tok, stride=blocks), :] = mine[:, c * LANES : (c + 1) * LANES]
        gath[core, i, y, ty] = pack_v[i].astype(BF16)
    in_grad.wait()
    lane_rows = lax.broadcasted_iota(jnp.int32, (rows, TILE, LANES), 1)

    def column(ref, first, side):
        base, row = ((0, 0), (cols - TILE, TILE - 1))[side]
        edge = ref[first : first + rows, base : base + TILE, :].astype(F32)
        return jnp.sum(jnp.where(lane_rows == row, edge, 0.0), axis=1)

    for side in range(2):
        col_send[side] = column(grad_v, 1, side).astype(BF16)

    col_halo[...] = jnp.zeros_like(col_halo)
    col_index = lax.broadcasted_iota(jnp.int32, (cols, LANES), 0)

    def shift_row(r, carry):
        line = grad_v[r]
        wide_line = line.astype(F32)
        before = jnp.where(col_index == 0, col_halo[0, pl.ds(r, 1)], pltpu.roll(wide_line, 1, 0))
        after = jnp.where(
            col_index == cols - 1, col_halo[1, pl.ds(r, 1)], pltpu.roll(wide_line, cols - 1, 0)
        )
        shifted[r, :, 0:LANES] = after.astype(BF16)
        shifted[r, :, LANES : 2 * LANES] = line
        shifted[r, :, 2 * LANES :] = before.astype(BF16)
        return carry

    lax.fori_loop(1, rows + 1, shift_row, 0)
    for r in (0, rows + 1):
        shifted[r] = jnp.zeros((cols, 3 * LANES), BF16)
    in_feat.wait()

    group = 4
    pixels = group * cols

    def neighbours(r):
        return jnp.concatenate(
            [
                shifted[pl.ds(r + 2 - ky, group)].reshape(pixels, 3 * LANES)
                for ky in range(3)
            ],
            axis=-1,
        )

    def silu(v):
        value = v.astype(F32)
        return (value * jax.nn.sigmoid(value)).astype(BF16)

    acc[...] = jnp.zeros_like(acc)

    def weight_step(i, carry):
        active = silu(feat_v[pl.ds(i * group, group)].reshape(pixels, LANES))
        acc[...] += dot(active, neighbours(i * group), TN)
        return carry

    lax.fori_loop(0, rows // group, weight_step, 0)
    for k in range(9):
        flat[k * LANES : (k + 1) * LANES, :] = acc[:, k * LANES : (k + 1) * LANES]
    for side in range(2):
        edge_row[side] = silu(feat_v[(0, rows - 1)[side]])
        edge_col[side] = silu(column(feat_v, 0, side))

    pl.semaphore_wait(barrier, len(peers))

    up, down = ty > 0, ty < d.ty - 1
    left, right = tx > 0, tx < d.tx - 1
    upper, lower = lax.rem(ty + d.ty - 1, d.ty), lax.rem(ty + 1, d.ty)
    row_up = send(grad_v.at[1], grad_v.at[rows + 1], "row", 0, 1, at_ty(upper))
    row_down = send(grad_v.at[rows], grad_v.at[0], "row", 1, 0, at_ty(lower))
    start(row_up, up)
    start(row_down, down)
    arrivals = []
    for side, there, out_ok, in_ok in (
        (0, lax.rem(tx + d.tx - 1, d.tx), left, right),
        (1, lax.rem(tx + 1, d.tx), right, left),
    ):
        for dy, there_y, out_y, in_y in (
            (0, upper, up, down),
            (1, ty, True, True),
            (2, lower, down, up),
        ):
            copy = send(
                col_send.at[side],
                col_recv.at[1 - side, 2 - dy],
                "col",
                side * 3 + dy,
                (1 - side) * 3 + 2 - dy,
                (rep, there_y, there),
            )
            start(copy, jnp.logical_and(out_ok, out_y))
            arrivals.append((jnp.logical_and(in_ok, in_y), copy, 1 - side, 2 - dy))

    def tok_z(i):
        mine = gath.at[core, :, y, ty]
        return send(mine, mine, "tok_z", i, ty, at_ty(lax.rem(ty + i, d.ty)))

    def tok_z_from(t):
        there = gath.at[core, :, y, t]
        return send(there, there, "tok_z", 0, t, at_ty(t))

    def tok_y(i, t):
        tile = gath.at[core, :, y, t]
        k = i * d.ty + t
        return send(tile, tile, "tok_y", k, k, at_tx(lax.rem(tx + i * CORES, d.tx)))

    for i in sorted(range(1, d.ty), key=lambda i: abs(2 * i - d.ty)):
        start(tok_z(i))
    for i in range(1, d.y):
        tok_y(i, ty).start()

    @pl.when(jnp.logical_not(up))
    def _():
        grad_v[0] = jnp.zeros((cols, LANES), BF16)

    @pl.when(jnp.logical_not(down))
    def _():
        grad_v[rows + 1] = jnp.zeros((cols, LANES), BF16)

    pl.when(up)(row_down.wait_recv)
    pl.when(down)(row_up.wait_recv)
    for ok, copy, side, place in arrivals:

        @pl.when(ok)
        def _(copy=copy, side=side, place=place):
            copy.wait_recv()
            tile = col_recv[side, place].astype(F32)
            if place == 0:
                col_halo[side, 0:1] = tile[rows - 1 : rows]
            elif place == 1:
                col_halo[side, 1 : rows + 1] = tile
            else:
                col_halo[side, rows + 1 : rows + 2] = tile[0:1]

    def add(k, term):
        flat[k * LANES : (k + 1) * LANES, :] += term

    for side, r, ky in ((0, 0, 2), (1, rows + 1, 0)):
        shift_row(r, 0)
        more = dot(edge_row[side], shifted[r], TN)
        for kx in range(3):
            add(ky * 3 + kx, more[:, kx * LANES : (kx + 1) * LANES])
    halo_row = lax.broadcasted_iota(jnp.int32, (rows + 8, LANES), 0)
    inside = jnp.logical_and(halo_row >= 1, halo_row <= rows)
    for side, kx in ((0, 2), (1, 0)):
        line = jnp.where(inside, col_halo[side], 0.0)
        three = jnp.concatenate([line[2 - ky : 2 - ky + rows] for ky in range(3)], axis=1)
        more = dot(edge_col[side], three.astype(BF16), TN)
        for ky in range(3):
            add(ky * 3 + kx, more[:, ky * LANES : (ky + 1) * LANES])

    def core_rows(c):
        return pl.ds(pl.multiple_of(c * d.half, TILE), d.half)

    core_send[...] = flat[core_rows(1 - core), :].astype(BF16)
    to_core = send(core_send, core_v, "core", 0, 0, other_core)
    start(to_core)

    tile_row = lax.broadcasted_iota(jnp.int32, (TILE, LANES), 0)

    def fix_row(r, carry):
        for side, base, lanes, row in ((0, 0, 2 * LANES, 0), (1, cols - TILE, 0, TILE - 1)):
            here = (r, pl.ds(base, TILE), pl.ds(lanes, LANES))
            tile = shifted[here].astype(F32)
            tile = jnp.where(tile_row == row, col_halo[side, pl.ds(r, 1)], tile)
            shifted[here] = tile.astype(BF16)
        return carry

    lax.fori_loop(1, rows + 1, fix_row, 0)

    to_core.wait_recv()
    half_v[...] = (flat[core_rows(core), :] + core_v[...].astype(F32)).astype(BF16)

    spare = lax.rem(chip + core * (d.chips - d.extra), d.chips)
    has_extra = spare < d.extra
    last = d.chips * d.piece

    def turned(e):
        return lax.rem(e + core * d.extra, d.chips)

    def rows_of(c):
        return pl.ds(pl.multiple_of(c * d.piece, TILE), d.piece)

    def tile_of(e):
        return pl.ds(pl.multiple_of(last + e * TILE, TILE), TILE)

    def to_plane(i):
        there = beside(i)
        return send(
            half_v.at[rows_of(there)], plane_v.at[chip], "plane", i, chip, at_chip(there)
        )

    def from_plane(i):
        there = beside(i)
        return send(
            half_v.at[rows_of(there)], plane_v.at[there], "plane", i, there, at_chip(there)
        )

    def to_plane_extra(e):
        there = turned(e)
        return send(
            half_v.at[tile_of(e)], plane_w.at[chip], "plane_extra", e, chip, at_chip(there)
        )

    def from_plane_extra(i):
        there = beside(i)
        return send(
            half_v.at[tile_of(0)], plane_w.at[there], "plane_extra", 0, there, at_chip(there)
        )

    for i in range(1, d.chips):
        start(to_plane(i))
    for e in range(d.extra):
        start(to_plane_extra(e), spare != e)

    for distance in range(1, d.ty):
        for t in (ty + distance, ty - distance):

            @pl.when(jnp.logical_and(t >= 0, t < d.ty))
            def _(t=t):
                tok_z_from(t).wait_recv()
                for i in range(1, d.y):
                    tok_y(i, t).start()

    def along_z(i):
        return send(z_v.at[z], z_v.at[z], "along_z", i, i, at_z(lax.rem(z + i, d.z)))

    def along_z_extra(i):
        return send(z_w.at[z], z_w.at[z], "along_z_extra", i, i, at_z(lax.rem(z + i, d.z)))

    def summed(ref, count):
        total = ref[0].astype(F32)
        for i in range(1, count):
            total = total + ref[i].astype(F32)
        return total.astype(BF16)

    plane_v[chip] = half_v[rows_of(chip), :]
    for i in range(1, d.chips):
        from_plane(i).wait_recv()
    z_v[z] = summed(plane_v, d.chips)
    for i in reversed(far):
        start(along_z(i))

    @pl.when(has_extra)
    def _():
        plane_w[chip] = half_v[tile_of(spare), :]
        for i in range(1, d.chips):
            from_plane_extra(i).wait_recv()
        z_w[z] = summed(plane_w, d.chips)
        for i in reversed(far):
            along_z_extra(i).start()

    for t in range(d.ty):
        for i in range(1, d.y):
            tok_y(i, t).wait_recv()
    to_core_tok = send(gath.at[core], gath.at[core], "tok_core", 0, 0, other_core)
    start(to_core_tok)

    share = d.tokens // CORES
    heads = d.width // CORES
    my_heads = pl.ds(pl.multiple_of(core * heads, LANES), heads)
    for copy in in_proj:
        copy.wait()
    for c in (core, 1 - core):
        here = pl.ds(pl.multiple_of(c * share, TILE), share)
        if c is not core:
            to_core_tok.wait_recv()
        for i in range(2):
            wide[...] = gath[c, i].reshape(share * blocks, LANES).astype(F32)
            for b in range(blocks):
                tok_all[i, here, b * LANES : (b + 1) * LANES] = wide[
                    pl.ds(b, share, stride=blocks), :
                ].astype(BF16)
        for i in range(3):
            qkv[here, i * heads : (i + 1) * heads] = dot(
                tok_all[0, here], proj_w[i, :, my_heads], NN
            ).astype(BF16)

    lane = lax.broadcasted_iota(jnp.int32, (d.tokens, LANES), 1)
    low = lane < HEAD_DIM
    scale = 1.0 / HEAD_DIM**0.5

    def head_pair(p, carry):
        def block(ref, offset):
            return ref[:, pl.ds(pl.multiple_of(offset + p * LANES, LANES), LANES)]

        def halves(v):
            zero = jnp.zeros_like(v)
            return jnp.concatenate([jnp.where(low, v, zero), jnp.where(low, zero, v)], axis=0)

        key = block(qkv, heads)
        value = block(qkv, 2 * heads)
        query2 = halves(block(qkv, 0))
        upstream2 = halves(block(tok_all.at[1], core * heads))
        scores = dot(key, query2, NT) * scale
        expos = jnp.exp(scores - jnp.max(scores, axis=0, keepdims=True))
        probs = expos / jnp.sum(expos, axis=0, keepdims=True)
        dprobs = dot(value, upstream2, NT)
        dscores = probs * (dprobs - jnp.sum(dprobs * probs, axis=0, keepdims=True))
        dscores_low = (dscores * scale).astype(BF16)
        value_grad = dot(probs.astype(BF16), upstream2, NN)
        key_grad = dot(dscores_low, query2, NN)
        both = dot(dscores_low, key, TN)
        query_grad = jnp.where(low, both[: d.tokens], both[d.tokens :])
        for i, g in enumerate((query_grad, key_grad, value_grad)):
            here = pl.ds(pl.multiple_of(i * heads + p * LANES, LANES), LANES)
            pgrad[:, here] = g.astype(BF16)
        return carry

    lax.fori_loop(0, heads // LANES, head_pair, 0)

    pick_row = lax.broadcasted_iota(jnp.int32, (2 * 8, d.width), 0)
    pick_col = lax.broadcasted_iota(jnp.int32, (2 * 8, d.width), 1)
    own_row = lax.broadcasted_iota(jnp.int32, (2 * 8, d.tokens), 0)
    own_col = lax.broadcasted_iota(jnp.int32, (2 * 8, d.tokens), 1)

    def rows_for(c):
        place = ((c * d.y + y) * d.ty + ty) * d.tok
        channel = (ty * d.tx + y * CORES + c) * (d.width // (d.ty * d.tx))
        pick = jnp.logical_and(pick_col == channel + pick_row, pick_row < 8).astype(F32)
        columns = dot(pick.astype(BF16), tok_all[0], NT)
        picked = jnp.where(own_row < 8, columns, (own_col == place + own_row - 8).astype(F32))
        return dot(picked.astype(BF16), pgrad[...], NN).astype(BF16)

    head_send[...] = rows_for(1 - core)
    to_core_heads = send(head_send, head_v.at[core], "heads", 0, 0, other_core)
    start(to_core_heads)
    head_v[core] = rows_for(core)
    to_core_heads.wait_recv()
    parts = [head_v[c].astype(F32) for c in range(CORES)]
    px_v[x] = jnp.concatenate([p[:8] for p in parts], axis=0).astype(BF16)

    def proj_x(i):
        there = (lax.rem(x + i, d.x) * d.zh + zh, ty, tx)
        return send(px_v.at[x], px_v.at[x], "proj_x", i, i, there)

    for i in range(1, d.x):
        start(proj_x(i))
    back = jnp.zeros((8, d.width), F32)
    for c in range(CORES):
        own_grads = parts[c][8:].astype(BF16)
        for i in range(3):
            back = back + dot(
                own_grads[:, i * heads : (i + 1) * heads],
                proj_w[i, :, c * heads : (c + 1) * heads],
                NT,
            )
    token_out[0] = (tok_v[1].astype(F32) + back[: d.tok]).astype(BF16)

    for copy in in_taps:
        copy.wait()

    def feature_step(i, carry):
        here = pl.ds(i * group, group)
        value = feat_v[here].reshape(pixels, LANES).astype(F32)
        gate = jax.nn.sigmoid(value)
        slope = gate * (1.0 + value * (1.0 - gate))
        act_grad = dot(neighbours(i * group), taps[...], NT)
        upstream = grad_v[pl.ds(i * group + 1, group)].reshape(pixels, LANES).astype(F32)
        feature_out[0, here] = (upstream + slope * act_grad).astype(BF16).reshape(group, cols, LANES)
        return carry

    lax.fori_loop(0, rows // group, feature_step, 0)

    for i in range(1, d.x):
        proj_x(i).wait_recv()
    pz_v[zh] = summed(px_v, d.x)
    proj_z = send(pz_v.at[zh], pz_v.at[zh], "proj_z", 0, 0, at_z(lax.rem(z + d.ty, d.z)))
    start(proj_z)

    def spread(c, i):
        here = weight_out.at[core, rows_of(c)]
        return send(here, here, "spread", i, c, at_chip(beside(i)))

    def spread_extra(e, i):
        here = weight_out.at[core, tile_of(e)]
        return send(here, here, "spread_extra", i, e, at_chip(beside(i)))

    for i in range(1, d.z):
        along_z(i).wait_recv()
    weight_out[core, rows_of(chip)] = summed(z_v, d.z)
    for i in range(1, d.chips):
        start(spread(chip, i))

    @pl.when(has_extra)
    def _():
        for i in range(1, d.z):
            along_z_extra(i).wait_recv()
        weight_out[core, tile_of(spare)] = summed(z_w, d.z)
        for i in range(1, d.chips):
            spread_extra(spare, i).start()

    for i in range(1, d.chips):
        spread(beside(i), 0).wait_recv()
    for e in range(d.extra):
        pl.when(spare != e)(spread_extra(e, 0).wait_recv)
    back_core = send(weight_out.at[core], weight_out.at[core], "core_back", 0, 0, other_core)
    start(back_core)

    proj_z.wait_recv()
    total = pz_v[0].astype(F32)
    for k in range(1, d.zh):
        total = total + pz_v[k].astype(F32)
    for i in range(3):
        for c in range(CORES):
            first = i * d.width + c * heads
            proj_out[:, first : first + heads] = total[c * 8 : c * 8 + 8, i * heads : (i + 1) * heads]

    back_core.wait_recv()

    for when, copy in sent:
        if when is None:
            copy.wait_send()
        else:
            pl.when(when)(copy.wait_send)

    @pl.when(has_extra)
    def _():
        for i in range(1, d.z):
            along_z_extra(i).wait_send()
        for i in range(1, d.chips):
            spread_extra(spare, i).wait_send()

    for t in range(d.ty):
        for i in range(1, d.y):
            tok_y(i, t).wait_send()


def outputs(feature, weight, token, proj, feature_out, weight_out, token_out, proj_out, high_v, sem):
    copies = [
        pltpu.make_async_copy(src, dst, sem.at[i])
        for i, (src, dst) in enumerate(
            ((feature, feature_out), (token, token_out), (proj, proj_out), (high_v, weight_out))
        )
    ]
    for copy in copies[:-1]:
        copy.start()
    high_v[...] = weight[...].astype(F32)
    copies[-1].start()
    for copy in copies:
        copy.wait()


def shards(d, *args):
    tile = (d.rows, d.cols, LANES)
    half = 3 * d.width // 2
    blocks = d.width // LANES
    packed = d.tok * blocks
    assert packed == TILE and d.rows == TILE
    _, messages = message_slots(d)
    hbm = pl.BlockSpec(memory_space=pl.ANY)
    vmem = pl.BlockSpec(memory_space=pltpu.VMEM)
    args = [pltpu.with_memory_space_constraint(a, pltpu.HBM) for a in args]
    results = pl.pallas_call(
        functools.partial(kernel, d),
        out_shape=(
            pltpu.VMEM((1, *tile), BF16),
            pltpu.VMEM((CORES, d.half, LANES), BF16),
            pltpu.VMEM((1, d.tok, d.width), BF16),
            pltpu.VMEM((8, 3 * d.width), F32),
        ),
        in_specs=[hbm] * 8,
        out_specs=(vmem,) * 4,
        scratch_shapes=[
            pltpu.VMEM(tile, BF16),
            pltpu.VMEM((d.rows + 2, d.cols, LANES), BF16),
            pltpu.VMEM((d.rows + 2, d.cols, 3 * LANES), BF16),
            pltpu.VMEM((LANES, 9 * LANES), BF16),
            pltpu.VMEM((3, d.width, d.width), BF16),
            pltpu.VMEM((LANES, 9 * LANES), F32),
            pltpu.VMEM((9 * LANES, LANES), F32),
            pltpu.VMEM((2, d.cols, LANES), BF16),
            pltpu.VMEM((2, d.rows, LANES), BF16),
            pltpu.VMEM((d.half, LANES), BF16),
            pltpu.VMEM((d.half, LANES), BF16),
            pltpu.VMEM((d.half, LANES), BF16),
            pltpu.VMEM((d.chips, d.piece, LANES), BF16),
            pltpu.VMEM((d.z, d.piece, LANES), BF16),
            pltpu.VMEM((d.chips, TILE, LANES), BF16),
            pltpu.VMEM((d.z, TILE, LANES), BF16),
            pltpu.VMEM((2, d.rows, LANES), BF16),
            pltpu.VMEM((2, 3, d.rows, LANES), BF16),
            pltpu.VMEM((2, d.rows + 8, LANES), F32),
            pltpu.VMEM((2, d.tok, d.width), BF16),
            pltpu.VMEM((2, packed, LANES), F32),
            pltpu.VMEM((CORES, 2, d.y, d.ty, packed, LANES), BF16),
            pltpu.VMEM((d.tokens * blocks // CORES, LANES), F32),
            pltpu.VMEM((2, d.tokens, d.width), BF16),
            pltpu.VMEM((d.tokens, half), BF16),
            pltpu.VMEM((d.tokens, half), BF16),
            pltpu.VMEM((2 * 8, half), BF16),
            pltpu.VMEM((CORES, 2 * 8, half), BF16),
            pltpu.VMEM((d.zh, 16, half), BF16),
            pltpu.VMEM((d.x, 16, half), BF16),
            pltpu.SemaphoreType.DMA((16,)),
            pltpu.SemaphoreType.DMA((messages,)),
            pltpu.SemaphoreType.DMA((messages,)),
        ],
        compiler_params=pltpu.CompilerParams(
            collective_id=0, has_side_effects=True, vmem_limit_bytes=VMEM_LIMIT
        ),
    )(*args)
    results = [pltpu.with_memory_space_constraint(r, pltpu.VMEM) for r in results]
    feature_grad, conv_weight_grad, token_grad, proj_grad = pl.pallas_call(
        outputs,
        out_shape=(
            jax.ShapeDtypeStruct((1, *tile), BF16),
            jax.ShapeDtypeStruct((CORES, d.half, LANES), F32),
            jax.ShapeDtypeStruct((1, d.tok, d.width), BF16),
            jax.ShapeDtypeStruct((8, 3 * d.width), F32),
        ),
        in_specs=[vmem] * 4,
        out_specs=(hbm,) * 4,
        scratch_shapes=[
            pltpu.VMEM((CORES, d.half, LANES), F32),
            pltpu.SemaphoreType.DMA((4,)),
        ],
        compiler_params=pltpu.CompilerParams(vmem_limit_bytes=VMEM_LIMIT),
    )(*results)
    return feature_grad, conv_weight_grad.reshape(3, 3, LANES, LANES), token_grad, proj_grad


def solution(mesh):
    sizes = mesh.shape
    zh = 2

    def whole(*args):
        _, height, width, _ = args[0].shape
        _, tokens, channels = args[3].shape
        d = Dims(
            x=sizes["rep"] // zh,
            zh=zh,
            ty=sizes["ty"],
            y=sizes["tx"] // CORES,
            rows=height // sizes["ty"],
            cols=width // sizes["tx"],
            tok=tokens // (sizes["ty"] * sizes["tx"]),
            width=channels,
        )
        in_specs = (
            P("rep", "ty", "tx", None),
            P("rep", "ty", "tx", None),
            P(),
            P("rep", ("ty", "tx"), None),
            P("rep", ("ty", "tx"), None),
            P(),
            P(),
            P(),
        )
        out_specs = (
            P("rep", "ty", "tx", None),
            P(),
            P("rep", ("ty", "tx"), None),
            P(("ty", "tx"), None),
        )
        return jax.shard_map(
            functools.partial(shards, d),
            mesh=mesh,
            in_specs=in_specs,
            out_specs=out_specs,
            check_vma=False,
        )(*args)

    return whole
```
